128 devices in a mesh: dp: 8 (over z_hi, x), tensor: 16 (over z_lo, y, core).
Axes of the slice: x: 4, y: 4, z: 4 (z_hi: 2, z_lo: 2; z = z_hi * 2 + z_lo), core: 2. Of those that a mesh axis runs over, the one named last changes fastest.
Arguments:
- partials: bfloat16 [16, 4096, 16384], P('tensor', 'dp'), parts along dimension 1, may hold values from -6 to 6
- residual: bfloat16 [4096, 16384], P(('dp', 'tensor')), parts along dimension 0, may hold values from -6 to 6
- norm_gain: bfloat16 [16384], replicated, may hold values from 0.099609375 to 1.8984375
- qkv_weight: bfloat16 [16384, 10240], P(None, 'tensor'), may hold values from -0.046875 to 0.046875
Outputs:
- new_stream: bfloat16 [4096, 16384], P(('dp', 'tensor')), parts along dimension 0
- projected: bfloat16 [4096, 10240], P('dp', 'tensor'), parts along dimension 0
The draws below stay inside these ranges and needn't reach their ends.
There are 8 independent parts, one for each index of `dp`. The reference program is written for one: setup_inputs(seed, part) draws one part's arguments, and reference() takes and returns one part's arrays. A program takes and returns all parts, laid end to end along the dimension named above; an argument that names none is the same for every part. Nothing has to cross between parts.
All inputs are finite; a program needn't handle non-finite values.
Results may differ from the reference program's by a relative error of at most 0.024.
Values may be sent and summed in bfloat16 or wider, within the bound.
No kernel may reach another device: no remote copies, remote signals or barrier semaphores. Data moves between devices by JAX's collectives and lax.ppermute only.
A program may use at most 256 MiB of HBM per device.

```python
import jax
import jax.numpy as jnp
from jax import lax

D = 16384
TOKENS = 512
QCOLS = 10240
N_TENSOR = 16


def spiked(array, own_key, source, target, blocks, factor):
    def block_of(position):
        return (jnp.arange(array.shape[position]) // (array.shape[position] // blocks)).reshape((-1,) + (1,) * (array.ndim - 1 - position))

    first = jax.random.permutation(own_key, blocks)[block_of(target)]
    far = (block_of(target) + blocks // 2) % blocks
    return jnp.where((block_of(source) == first) | (block_of(source) == far), factor * array, array)


def level_of(key, shape, cuts, low, top_value):
    loudness = 1.0
    for dim, blocks in cuts:
        steps = jax.random.uniform(jax.random.fold_in(jax.random.fold_in(key, 6), dim), (blocks,), jnp.float32, low / len(cuts), top_value / len(cuts))
        loudness = loudness * jnp.repeat(jnp.exp(steps), shape[dim] // blocks).reshape((-1,) + (1,) * (len(shape) - 1 - dim))
    return loudness


def bell_draw(rng, extent, deviation, limit, cuts=(), dtype=jnp.bfloat16):
    array = deviation * jax.random.normal(rng, extent, jnp.float32)
    if cuts:
        array = array * level_of(rng, extent, cuts, -0.22, 0.18)
    return jnp.clip(array, -limit, limit).astype(dtype)


def bell_draw_with(own_key, extent, deviation, bound, split, heavy, held_as=jnp.bfloat16):
    array = deviation * jax.random.normal(own_key, extent, jnp.float32)
    if split:
        array = array * level_of(own_key, extent, split, -0.22, 0.18)
    return jnp.clip(spiked(array, jax.random.fold_in(own_key, 3), *heavy), -bound, bound).astype(held_as)


def setup_inputs(seed: int = 0, part: int = 0) -> dict:
    arg_keys = jax.random.split(jax.random.key(seed), 5)
    part_keys = jax.random.split(jax.random.fold_in(arg_keys[4], part), 5)
    partials = bell_draw_with(part_keys[0], (N_TENSOR, TOKENS, D), 0.5, 6.0, ((0, 16),), (0, 1, 16, 2.0))
    residual = bell_draw(part_keys[1], (TOKENS, D), 1.0, 6.0, ((0, 16),))
    norm_gain = jnp.clip(1.0 + 0.18 * jax.random.normal(arg_keys[2], (D,), jnp.float32), 0.099609375, 1.8984375).astype(jnp.bfloat16)
    qkv_weight = bell_draw(arg_keys[3], (D, QCOLS), D ** -0.5, 0.046875, ((1, 16),))
    return {"partials": partials, "residual": residual, "norm_gain": norm_gain, "qkv_weight": qkv_weight}


def reference(partials, residual, norm_gain, qkv_weight):
    summed = lax.optimization_barrier(jnp.sum(partials.astype(jnp.float32), axis=0))
    stream = residual.astype(jnp.float32) + summed
    meansq = lax.optimization_barrier(jnp.mean(stream * stream, axis=-1, keepdims=True))
    normed = (stream * lax.rsqrt(meansq + 1e-05) * norm_gain.astype(jnp.float32)).astype(jnp.bfloat16)
    projected = jnp.dot(normed, qkv_weight, preferred_element_type=jnp.float32)
    return (stream.astype(jnp.bfloat16), projected.astype(jnp.bfloat16))
```

```python
import functools

import jax
import jax.numpy as jnp
from jax import lax
from jax.experimental import pallas as pl
from jax.experimental.pallas import tpu as pltpu
from jax.sharding import PartitionSpec as P

NZ, NY, NC = 2, 4, 2
ROWS = 32
D = 16384
COLS = 640
STEP = 256
NOTE = 128
ANY = pl.BlockSpec(memory_space=pl.ANY)
HBM = pl.BlockSpec(memory_space=pltpu.HBM)
SMEM = pl.BlockSpec(memory_space=pltpu.SMEM)
VMEM = pl.BlockSpec(memory_space=pltpu.VMEM)
VMEM_BYTES = 48 * 1024 * 1024


def index_of(z, y, c):
    return (z * NY + y % NY) * NC + c


def pairs(move):
    return [
        (index_of(z, y, c), index_of(*move(z, y, c)))
        for z in range(NZ)
        for y in range(NY)
        for c in range(NC)
    ]


MOVES = {"a": (0, 1), "b": (0, 3), "z": (1, 0)}
TO = {d: pairs(lambda z, y, c, m=m: (z ^ m[0], y ^ m[1], c)) for d, m in MOVES.items()}
TO_CORE = pairs(lambda z, y, c: (z, y, 1 - c))


def send(x, where):
    return lax.ppermute(x, "tensor", where)


def bf16(x):
    return x.astype(jnp.bfloat16)


def shape(*dims, dtype=jnp.bfloat16):
    return jax.ShapeDtypeStruct(dims, dtype)


class Copies:
    def __init__(self, sems):
        self.sems, self.count = sems, 0

    def start(self, source, target):
        copy = pltpu.make_async_copy(source, target, self.sems.at[self.count])
        self.count += 1
        copy.start()
        return copy


def by_columns(width, body):
    steps = width // STEP
    unroll = next(u for u in (3, 7, 5, 2, 1) if steps % u == 0)

    def at(i, carry):
        return body(pl.ds(pl.multiple_of(i * STEP, STEP), STEP), carry)

    return functools.partial(lax.fori_loop, 0, steps, at, unroll=unroll)


def total_of(sources, columns):
    total = sources[0][:, columns].astype(jnp.float32)
    for ref in sources[1:]:
        total = total + ref[:, columns].astype(jnp.float32)
    return total


def call(name, kernel, ins, outs, scratch, copies, after, aliases={}, pinned=()):
    return pl.pallas_call(
        kernel,
        in_specs=[SMEM]
        + [HBM if i in pinned else ANY for i in range(1, len(ins))]
        + [ANY] * len(after),
        out_specs=[ANY] * len(outs),
        name=name,
        out_shape=outs,
        scratch_shapes=scratch + [pltpu.SemaphoreType.DMA((copies,))],
        input_output_aliases=aliases,
        compiler_params=pltpu.CompilerParams(vmem_limit_bytes=VMEM_BYTES),
        cost_estimate=pl.CostEstimate(flops=0, bytes_accessed=1024, transcendentals=0),
    )(*ins, *after)


def copied(name, ins, outs, items, after, pinned=()):
    n = len(ins)

    def kernel(*refs):
        place, sources = refs[0], refs[1:n]
        targets, sems = refs[n + len(after) : -1], refs[-1]
        copies = Copies(sems)
        going = [
            copies.start(source, targets[k].at[index])
            for k, index, source in items(place, sources)
        ]
        for copy in going:
            copy.wait()

    return call(name, kernel, ins, outs, [], 36, after, pinned=pinned)


def added(name, ins, outs, items, after):
    n = len(ins)
    plan = items(None, [None] * (n - 1))
    most = max(len(sources) for _, _, sources, _ in plan)
    widest = max(width for _, _, _, width in plan)

    def kernel(*refs):
        place, sources = refs[0], refs[1:n]
        targets = refs[n + len(after) : n + len(after) + len(outs)]
        taken, made, sems = refs[-3:]
        copies = Copies(sems)
        todo, storing = [], []
        for i, (k, index, blocks, width) in enumerate(items(place, sources)):
            slots = [taken.at[i, j, :, pl.ds(0, width)] for j in range(len(blocks))]
            loads = [copies.start(b, s) for b, s in zip(blocks, slots)]
            todo.append((k, index, slots, loads, width))
        for i, (k, index, slots, loads, width) in enumerate(todo):
            for copy in loads:
                copy.wait()

            def body(columns, carry, i=i, slots=slots):
                made[i, :, columns] = bf16(total_of(slots, columns))
                return carry

            by_columns(width, body)(0)
            here = made.at[i, :, pl.ds(0, width)]
            storing.append(copies.start(here, targets[k].at[index]))
        for copy in storing:
            copy.wait()

    scratch = [
        pltpu.VMEM((len(plan), most, ROWS, widest), jnp.bfloat16),
        pltpu.VMEM((len(plan), ROWS, widest), jnp.bfloat16),
    ]
    return call(name, kernel, ins, outs, scratch, len(plan) * (most + 1), after, pinned=(1,))


class Part:
    def __init__(self, start, features, dims, note=0):
        self.start, self.features, self.note = start, features, note
        self.sent = features + note
        self.columns = pl.ds(start, features)
        self.dims = dims

    def apart(self, *steps):
        z = y = 0
        for d, step in zip(self.dims, steps):
            if step:
                z, y = z ^ MOVES[d][0], y ^ MOVES[d][1]
        return z, y


class Stream:
    def __init__(self, *parts):
        self.parts = parts
        self.start = parts[0].start
        self.features = sum(p.features for p in parts)
        self.note = sum(p.note for p in parts)

    def sent(self, part):
        return pl.ds(part.start - self.start, part.sent)


def row_block(place, apart):
    z, y = place[0], place[1]
    return lax.bitwise_xor(z, apart[0]) * NY + lax.bitwise_xor(y, apart[1])


def block(place, apart, dc):
    c = place[2]
    return row_block(place, apart) * NC + lax.bitwise_xor(c, dc)


def give(place, terms, wanted, after):
    width = sum(stream.features for stream, _ in wanted)

    def items(at, refs):
        (x,) = refs
        found, offset = [], 0
        for stream, first in wanted:
            for part in stream.parts:
                to = pl.ds(offset + part.start - stream.start, part.features)
                found += [
                    (
                        0,
                        (e2 * 2 + e3, slice(None), to),
                        x.at[block(at, part.apart(first, e2, e3), 1), :, part.columns],
                    )
                    for e2 in (1, 0)
                    for e3 in (0, 1)
                ]
            offset += stream.features
        return found

    count = 4 * sum(len(stream.parts) for stream, _ in wanted)

    def kernel(*refs):
        at, x = refs[:2]
        target, held, sems = refs[-3:]
        copies = Copies(sems)
        todo = []
        for _, index, source in items(at, (x,)):
            todo.append((index, copies.start(source, held.at[index])))
        storing = []
        for index, copy in todo:
            copy.wait()
            storing.append(copies.start(held.at[index], target.at[index]))
        for copy in storing:
            copy.wait()

    scratch = [pltpu.VMEM((4, ROWS, width), jnp.bfloat16)]
    out = shape(4, ROWS, width)
    return call("give", kernel, [place, terms], [out], scratch, 2 * count, after, pinned=(1,))


def pair_sum(at, x, r, offset, part, e1, e2, e3):
    if x is None:
        return [None, None]
    mine = x.at[block(at, part.apart(e1, e2, e3), 0), :, part.columns]
    return [mine, r.at[e2 * 2 + e3, :, pl.ds(offset + part.start, part.features)]]


def pick(ref, index):
    return None if ref is None else ref.at[index]


def first_step(place, terms, got, offset, stream, after):
    def items(at, refs):
        return [
            (k, e2 * 2 + e3, pair_sum(at, refs[0], refs[1], offset, part, 1, e2, e3), part.features)
            for k, part in enumerate(stream.parts)
            for e2 in (1, 0)
            for e3 in (0, 1)
        ]

    outs = [shape(4, ROWS, part.features) for part in stream.parts]
    return added("first", [place, terms, got], outs, items, after)


def second_step(place, terms, rest, one, stream, after):
    def items(at, refs):
        x, r, v = refs[0], refs[1], refs[2:5]
        return [
            (k, e3, pair_sum(at, x, r, 0, part, 0, 1, e3) + [pick(v[k], 2 + e3)], part.features)
            for k, part in enumerate(stream.parts)
            for e3 in (0, 1)
        ]

    outs = [shape(2, ROWS, part.features) for part in stream.parts]
    return added("second", [place, terms, rest, *one], outs, items, after)


def third_step(place, terms, rest, one, two, stream, after):
    def items(at, refs):
        x, r, v, w = refs[0], refs[1], refs[2:5], refs[5:8]
        return [
            (
                k,
                slice(None),
                pair_sum(at, x, r, 0, part, 0, 0, 1) + [pick(v[k], 1), pick(w[k], 1)],
                part.features,
            )
            for k, part in enumerate(stream.parts)
        ]

    outs = [shape(ROWS, part.features) for part in stream.parts]
    return added("third", [place, terms, rest, *one, *two], outs, items, after)


def finish(place, terms, rest, one, two, three, stream, residual, gain, so_far, after):
    ins = [place, terms, rest, *one, *two, *three, residual, gain, *so_far]
    widest = max(part.features for part in stream.parts)
    there = pl.ds(stream.start, stream.features)

    def kernel(*refs):
        at, x = refs[0], refs[1]
        r, v, w, u = refs[2], refs[3:6], refs[6:9], refs[9:12]
        residual_ref, gain_ref = refs[12:14]
        base = len(ins) + len(after)
        stream_out, gained_out, squares_out = refs[base], refs[base + 1 : base + 4], refs[base + 4]
        taken, old, gains, news, made, sums, sems = refs[base + 5 :]
        copies = Copies(sems)
        first = [
            copies.start(residual_ref.at[:, there], old),
            copies.start(gain_ref.at[:, there], gains),
        ]
        if so_far:
            first.append(copies.start(refs[15], sums))
        else:
            sums[...] = jnp.zeros_like(sums)
        loads, slots = [], []
        for k, part in enumerate(stream.parts):
            blocks = pair_sum(at, x, r, 0, part, 0, 0, 0)
            blocks = blocks + [v[k].at[0], w[k].at[0], u[k]]
            slots.append([taken.at[k, j, :, pl.ds(0, part.features)] for j in range(5)])
            loads.append([copies.start(b, s) for b, s in zip(blocks, slots[k])])
        for copy in first:
            copy.wait()
        total = sums[...]
        storing = []
        for k, part in enumerate(stream.parts):
            for copy in loads[k]:
                copy.wait()

            def body(columns, carry, k=k, offset=part.start - stream.start):
                here = pl.ds(pl.multiple_of(offset + columns.start, 128), STEP)
                x = total_of(slots[k], columns) + old[:, here].astype(jnp.float32)
                news[:, here] = bf16(x)
                made[k, :, columns] = bf16(x * gains[:, here])
                square = x * x
                return carry + square[:, :128] + square[:, 128:]

            total = by_columns(part.features, body)(total)
            if not part.note:
                here = made.at[k, :, pl.ds(0, part.features)]
                storing.append(copies.start(here, gained_out[k]))
        sums[...] = total
        storing.append(copies.start(news, stream_out.at[:, there]))
        storing.append(copies.start(sums, squares_out))
        for k, part in enumerate(stream.parts):
            if part.note:
                mean = jnp.sum(total, axis=1, keepdims=True) / D
                scale = jnp.broadcast_to(lax.rsqrt(mean + 1e-05), (ROWS, NOTE))
                high = bf16(scale).astype(jnp.float32)
                middle = bf16(scale - high).astype(jnp.float32)
                low = scale - high - middle
                lane = lax.broadcasted_iota(jnp.int32, (ROWS, NOTE), 1)
                parts = jnp.where(lane == 0, high, jnp.where(lane == 1, middle, low))
                made[k, :, pl.ds(part.features, NOTE)] = bf16(jnp.where(lane < 3, parts, 0.0))
                here = made.at[k, :, pl.ds(0, part.sent)]
                storing.append(copies.start(here, gained_out[k]))
        for copy in storing:
            copy.wait()

    outs = [shape(ROWS, D)]
    outs += [shape(ROWS, part.sent) for part in stream.parts]
    outs += [shape(ROWS, 128, dtype=jnp.float32)]
    scratch = [
        pltpu.VMEM((3, 5, ROWS, widest), jnp.bfloat16),
        pltpu.VMEM((ROWS, stream.features), jnp.bfloat16),
        pltpu.VMEM((1, stream.features), jnp.float32),
        pltpu.VMEM((ROWS, stream.features), jnp.bfloat16),
        pltpu.VMEM((3, ROWS, widest + NOTE), jnp.bfloat16),
        pltpu.VMEM((ROWS, 128), jnp.float32),
    ]
    aliases = {14: 0} if so_far else {}
    out = call("finish", kernel, ins, outs, scratch, 3 * 5 + 8, after, aliases, pinned=(1,))
    return out[1:4], (out[0], out[4])


def two_blocks(place, own, far, stream, after):
    def items(at, refs):
        return [(k, e, refs[e * 3 + k]) for e in range(2) for k in range(3)]

    outs = [shape(2, ROWS, part.sent) for part in stream.parts]
    return copied("two", [place, *own, *far], outs, items, after)


def four_blocks(place, near, far, stream, after):
    def items(at, refs):
        found = []
        for k, part in enumerate(stream.parts):
            for e in range(2):
                some = pl.ds(2 * e, 2)
                found.append((k, some, refs[e * 3 + k]))
                found.append((3, (some, slice(None), stream.sent(part)), refs[e * 3 + k]))
        return found

    outs = [shape(4, ROWS, part.sent) for part in stream.parts]
    outs.append(shape(4, ROWS, stream.features + stream.note))
    out = copied("four", [place, *near, *far], outs, items, after)
    return out[:3], out[3]


def multiplied(place, near, far, beside, other_far, weight, total, stream, depth, after):
    tiles = stream.features // depth
    slots = 2
    last = bool(stream.note)
    half = NC * NZ * NY * ROWS // 2
    ins = [*near, *far, beside, *other_far]
    more = [] if total is None else [total]

    def kernel(place_ref, *refs):
        sources, weight_ref = refs[:10], refs[10]
        total_ref = None if total is None else refs[11]
        at = 11 + len(more) + len(after)
        result = refs[at]
        rows, held, sems = refs[at + 1], refs[at + 2], refs[-1]
        out = refs[at + 3] if last else result
        copies = Copies(sems)

        def load(t):
            there = pl.ds(stream.start + t * depth, depth)
            return copies.start(weight_ref.at[there], held.at[t % slots])

        loads = [load(t) for t in range(slots)]
        taking = []
        for k, part in enumerate(stream.parts):
            columns = stream.sent(part)
            for e2 in range(2):
                for e3 in range(2):
                    e = e2 * 2 + e3
                    blocks = (
                        (0, 0, sources[k].at[e]),
                        (0, 1, sources[6].at[e, :, columns]),
                        (1, 0, sources[3 + k].at[e]),
                        (1, 1, sources[7 + k].at[e]),
                    )
                    for e1, c, source in blocks:
                        z, y = part.apart(e1, e2, e3)
                        to = pl.ds(((z * NY + y) * NC + c) * ROWS, ROWS)
                        taking.append(copies.start(source, rows.at[to, columns]))
        for copy in taking:
            copy.wait()
        for t in range(tiles):
            loads[t].wait()
            here = pl.ds(t * depth, depth)
            for m in range(2):
                some = pl.ds(m * half, half)
                product = jnp.dot(
                    rows[some, here], held[t % slots], preferred_element_type=jnp.float32
                )
                if t == 0:
                    out[some, :] = product if total_ref is None else total_ref[some, :] + product
                else:
                    out[some, :] += product
            if t + slots < tiles:
                loads.append(load(t + slots))
        if last:
            for z in range(NZ):
                for y in range(NY):
                    for c in range(NC):
                        to = row_block(place_ref, (z, y)) * NC + lax.bitwise_xor(place_ref[2], c)
                        to = pl.ds(pl.multiple_of(to * ROWS, ROWS), ROWS)
                        here = pl.ds(((z * NY + y) * NC + c) * ROWS, ROWS)
                        note = rows[here, pl.ds(stream.features, NOTE)].astype(jnp.float32)
                        scale = jnp.sum(note, axis=1, keepdims=True)
                        result[to, :] = bf16(out[here, :] * scale)

    dtype = jnp.bfloat16 if last else jnp.float32
    scratch = [
        pltpu.VMEM((2 * half, stream.features + stream.note), jnp.bfloat16),
        pltpu.VMEM((slots, depth, COLS), jnp.bfloat16),
    ]
    if last:
        scratch.append(pltpu.VMEM((2 * half, COLS), jnp.float32))
    return pl.pallas_call(
        kernel,
        in_specs=[SMEM] + [ANY] * 10 + [HBM] + [VMEM] * len(more) + [ANY] * len(after),
        name="multiply",
        out_specs=VMEM,
        out_shape=shape(2 * half, COLS, dtype=dtype),
        scratch_shapes=scratch + [pltpu.SemaphoreType.DMA((48 + tiles,))],
        compiler_params=pltpu.CompilerParams(vmem_limit_bytes=VMEM_BYTES),
        cost_estimate=pl.CostEstimate(flops=0, bytes_accessed=1024, transcendentals=0),
    )(place, *ins, weight, *more, *after)


ORDERS = (("a", "b", "z"), ("b", "z", "a"), ("z", "a", "b"))


def stream_of(start, sizes, note):
    parts = []
    for i, (size, dims) in enumerate(zip(sizes, ORDERS)):
        parts.append(Part(start, size, dims, note if i == len(sizes) - 1 else 0))
        start += size
    return Stream(*parts)


FIRST = stream_of(0, (3072, 3072, 3072), 0)
SECOND = stream_of(9216, (2304, 2304, 2560), NOTE)


def per_device(partials, residual, norm_gain, qkv_weight):
    t = lax.axis_index("tensor")
    core, y, z = t % 2, (t // 2) % 4, t // 8
    place = jnp.stack([z, y, core]).astype(jnp.int32)
    terms = partials.reshape(NZ * NY * NC, ROWS, D)
    gain = norm_gain.astype(jnp.float32).reshape(1, D)

    def along(step, arrays):
        return [send(x, TO[ORDERS[k][step]]) for k, x in enumerate(arrays)]

    def across(arrays):
        return [send(x, TO_CORE) for x in arrays]

    a, b = FIRST, SECOND
    a_give = give(place, terms, [(a, 1)], [])
    a_got = across(a_give)[0]
    give_rest = give(place, terms, [(a, 0), (b, 0), (b, 1)], [a_give[0]])
    give_rest, _ = lax.optimization_barrier((give_rest[0], a_got))
    rest = send(give_rest, TO_CORE)
    a_out = first_step(place, terms, a_got, 0, a, [give_rest])
    a_one = along(0, a_out)
    b_out = first_step(place, terms, rest, D - b.start, b, [a_out[0]])
    b_one = along(0, b_out)
    a_out = second_step(place, terms, rest, a_one, a, [b_out[0]])
    a_two = along(1, a_out)
    b_out = second_step(place, terms, rest, b_one, b, [a_out[0]])
    b_two = along(1, b_out)
    a_out = third_step(place, terms, rest, a_one, a_two, a, [b_out[0]])
    a_three = along(2, a_out)
    b_out = third_step(place, terms, rest, b_one, b_two, b, [a_out[0]])
    b_three = along(2, b_out)
    a_rows, so_far = finish(
        place, terms, rest, a_one, a_two, a_three, a, residual, gain, (), [b_out[0]]
    )
    a_far = along(2, a_rows)
    b_rows, (stream, _) = finish(
        place, terms, rest, b_one, b_two, b_three, b, residual, gain, so_far, []
    )
    b_far = along(2, b_rows)
    a_near = two_blocks(place, a_rows, a_far, a, [b_rows[0]])
    a_far = along(1, a_near)
    b_near = two_blocks(place, b_rows, b_far, b, [a_near[0]])
    b_far = along(1, b_near)
    a_near, a_beside = four_blocks(place, a_near, a_far, a, [b_near[0]])
    a_far = along(0, a_near)
    a_beside = send(a_beside, TO_CORE)
    b_near, b_beside = four_blocks(place, b_near, b_far, b, [a_near[0]])
    b_far = along(0, b_near)
    b_beside = send(b_beside, TO_CORE)

    a_all = (a_near, a_far, a_beside, across(a_far))
    total = multiplied(place, *a_all, qkv_weight, None, a, 1536, [b_near[0]])
    b_all = (b_near, b_far, b_beside, across(b_far))
    return stream, multiplied(place, *b_all, qkv_weight, total, b, 1792, [])


def solution(mesh):
    in_specs = (P("tensor", "dp", None), P(("dp", "tensor"), None), P(), P(None, "tensor"))
    out_specs = (P(("dp", "tensor"), None), P("dp", "tensor"))
    return jax.shard_map(
        per_device, mesh=mesh, in_specs=in_specs, out_specs=out_specs, check_vma=False
    )
```

```python
import functools

import jax
import jax.numpy as jnp
from jax import lax
from jax.experimental import pallas as pl
from jax.experimental.pallas import tpu as pltpu
from jax.sharding import PartitionSpec as P

NZ, NY, NC = 2, 4, 2
ROWS = 32
D = 16384
COLS = 640
STEP = 256
NOTE = 128
ANY = pl.BlockSpec(memory_space=pl.ANY)
SMEM = pl.BlockSpec(memory_space=pltpu.SMEM)
VMEM = pl.BlockSpec(memory_space=pltpu.VMEM)
MIB = 1024 * 1024
SUM_BYTES = 45 * MIB
ROW_BYTES = 16 * MIB
PRODUCT_BYTES = 41 * MIB


def index_of(z, y, c):
    return (z * NY + y % NY) * NC + c


def pairs(move):
    return [
        (index_of(z, y, c), index_of(*move(z, y, c)))
        for z in range(NZ)
        for y in range(NY)
        for c in range(NC)
    ]


MOVES = {"a": (0, 1), "b": (0, 3), "z": (1, 0)}
TO = {d: pairs(lambda z, y, c, m=m: (z ^ m[0], y ^ m[1], c)) for d, m in MOVES.items()}
TO_CORE = pairs(lambda z, y, c: (z, y, 1 - c))


def send(x, where):
    return lax.ppermute(x, "tensor", where)


def bf16(x):
    return x.astype(jnp.bfloat16)


def shape(*dims, dtype=jnp.bfloat16):
    return jax.ShapeDtypeStruct(dims, dtype)


class Copies:
    def __init__(self, sems):
        self.sems, self.count = sems, 0

    def start(self, source, target):
        copy = pltpu.make_async_copy(source, target, self.sems.at[self.count])
        self.count += 1
        copy.start()
        return copy


def by_columns(width, body):
    steps = width // STEP
    unroll = next(u for u in (3, 7, 5, 2, 1) if steps % u == 0)

    def at(i, carry):
        return body(pl.ds(pl.multiple_of(i * STEP, STEP), STEP), carry)

    return functools.partial(lax.fori_loop, 0, steps, at, unroll=unroll)


def total_of(sources, columns):
    total = sources[0][:, columns].astype(jnp.float32)
    for ref in sources[1:]:
        total = total + ref[:, columns].astype(jnp.float32)
    return total


def call(name, kernel, ins, outs, scratch, copies, after, aliases={}, limit=SUM_BYTES):
    return pl.pallas_call(
        kernel,
        in_specs=[SMEM] + [ANY] * (len(ins) - 1 + len(after)),
        out_specs=[ANY] * len(outs),
        name=name,
        out_shape=outs,
        scratch_shapes=scratch + [pltpu.SemaphoreType.DMA((copies,))],
        input_output_aliases=aliases,
        compiler_params=pltpu.CompilerParams(vmem_limit_bytes=limit),
        cost_estimate=pl.CostEstimate(flops=0, bytes_accessed=1024, transcendentals=0),
    )(*ins, *after)


def copied(name, ins, outs, items, after):
    n = len(ins)

    def kernel(*refs):
        place, sources = refs[0], refs[1:n]
        targets, sems = refs[n + len(after) : -1], refs[-1]
        copies = Copies(sems)
        going = [
            copies.start(source, targets[k].at[index])
            for k, index, source in items(place, sources)
        ]
        for copy in going:
            copy.wait()

    return call(name, kernel, ins, outs, [], 36, after, limit=ROW_BYTES)


def added(name, ins, outs, items, after):
    n = len(ins)
    plan = items(None, [None] * (n - 1))
    most = max(len(sources) for _, _, sources, _ in plan)
    widest = max(width for _, _, _, width in plan)

    def kernel(*refs):
        place, sources = refs[0], refs[1:n]
        targets = refs[n + len(after) : n + len(after) + len(outs)]
        taken, made, sems = refs[-3:]
        copies = Copies(sems)
        todo, storing = [], []
        for i, (k, index, blocks, width) in enumerate(items(place, sources)):
            slots = [taken.at[i, j, :, pl.ds(0, width)] for j in range(len(blocks))]
            loads = [copies.start(b, s) for b, s in zip(blocks, slots)]
            todo.append((k, index, slots, loads, width))
        for i, (k, index, slots, loads, width) in enumerate(todo):
            for copy in loads:
                copy.wait()

            def body(columns, carry, i=i, slots=slots):
                made[i, :, columns] = bf16(total_of(slots, columns))
                return carry

            by_columns(width, body)(0)
            here = made.at[i, :, pl.ds(0, width)]
            storing.append(copies.start(here, targets[k].at[index]))
        for copy in storing:
            copy.wait()

    scratch = [
        pltpu.VMEM((len(plan), most, ROWS, widest), jnp.bfloat16),
        pltpu.VMEM((len(plan), ROWS, widest), jnp.bfloat16),
    ]
    return call(name, kernel, ins, outs, scratch, len(plan) * (most + 1), after)


class Part:
    def __init__(self, start, features, dims, note=0):
        self.start, self.features, self.note = start, features, note
        self.sent = features + note
        self.columns = pl.ds(start, features)
        self.dims = dims

    def apart(self, *steps):
        z = y = 0
        for d, step in zip(self.dims, steps):
            if step:
                z, y = z ^ MOVES[d][0], y ^ MOVES[d][1]
        return z, y


class Stream:
    def __init__(self, parts, before):
        self.parts = parts
        self.start = parts[0].start
        self.features = sum(p.features for p in parts)
        self.note = sum(p.note for p in parts)
        self.before = before

    def sent(self, part):
        return pl.ds(part.start - self.start, part.sent)

    def place_of(self, k):
        return pl.ds(self.before[k], self.parts[k].sent)


def row_block(place, apart):
    z, y = place[0], place[1]
    return lax.bitwise_xor(z, apart[0]) * NY + lax.bitwise_xor(y, apart[1])


def block(place, apart, dc):
    c = place[2]
    return row_block(place, apart) * NC + lax.bitwise_xor(c, dc)


def give(place, terms, wanted, after):
    width = sum(stream.features for stream, _ in wanted)

    def items(at, refs):
        (x,) = refs
        found, offset = [], 0
        for stream, first in wanted:
            for part in stream.parts:
                to = pl.ds(offset + part.start - stream.start, part.features)
                found += [
                    (
                        0,
                        (e2 * 2 + e3, slice(None), to),
                        x.at[block(at, part.apart(first, e2, e3), 1), :, part.columns],
                    )
                    for e2 in (1, 0)
                    for e3 in (0, 1)
                ]
            offset += stream.features
        return found

    count = 4 * sum(len(stream.parts) for stream, _ in wanted)

    def kernel(*refs):
        at, x = refs[:2]
        target, held, sems = refs[-3:]
        copies = Copies(sems)
        todo = []
        for _, index, source in items(at, (x,)):
            todo.append((index, copies.start(source, held.at[index])))
        storing = []
        for index, copy in todo:
            copy.wait()
            storing.append(copies.start(held.at[index], target.at[index]))
        for copy in storing:
            copy.wait()

    scratch = [pltpu.VMEM((4, ROWS, width), jnp.bfloat16)]
    out = shape(4, ROWS, width)
    return call("give", kernel, [place, terms], [out], scratch, 2 * count, after)


def pair_sum(at, x, r, offset, part, e1, e2, e3):
    if x is None:
        return [None, None]
    mine = x.at[block(at, part.apart(e1, e2, e3), 0), :, part.columns]
    return [mine, r.at[e2 * 2 + e3, :, pl.ds(offset + part.start, part.features)]]


def pick(ref, index):
    return None if ref is None else ref.at[index]


def first_step(place, terms, got, offset, stream, after):
    def items(at, refs):
        return [
            (k, e2 * 2 + e3, pair_sum(at, refs[0], refs[1], offset, part, 1, e2, e3), part.features)
            for k, part in enumerate(stream.parts)
            for e2 in (1, 0)
            for e3 in (0, 1)
        ]

    outs = [shape(4, ROWS, part.features) for part in stream.parts]
    return added("first", [place, terms, got], outs, items, after)


def second_step(place, terms, rest, one, stream, after):
    def items(at, refs):
        x, r, v = refs[0], refs[1], refs[2:5]
        return [
            (k, e3, pair_sum(at, x, r, 0, part, 0, 1, e3) + [pick(v[k], 2 + e3)], part.features)
            for k, part in enumerate(stream.parts)
            for e3 in (0, 1)
        ]

    outs = [shape(2, ROWS, part.features) for part in stream.parts]
    return added("second", [place, terms, rest, *one], outs, items, after)


def third_step(place, terms, rest, one, two, stream, after):
    def items(at, refs):
        x, r, v, w = refs[0], refs[1], refs[2:5], refs[5:8]
        return [
            (
                k,
                slice(None),
                pair_sum(at, x, r, 0, part, 0, 0, 1) + [pick(v[k], 1), pick(w[k], 1)],
                part.features,
            )
            for k, part in enumerate(stream.parts)
        ]

    outs = [shape(ROWS, part.features) for part in stream.parts]
    return added("third", [place, terms, rest, *one, *two], outs, items, after)


def finish(place, terms, rest, one, two, three, stream, residual, gain, so_far, after):
    ins = [place, terms, rest, *one, *two, *three, residual, gain, *so_far]
    widest = max(part.features for part in stream.parts)
    there = pl.ds(stream.start, stream.features)

    def kernel(*refs):
        at, x = refs[0], refs[1]
        r, v, w, u = refs[2], refs[3:6], refs[6:9], refs[9:12]
        residual_ref, gain_ref = refs[12:14]
        base = len(ins) + len(after)
        stream_out, gained_out, squares_out = refs[base], refs[base + 1 : base + 4], refs[base + 4]
        taken, old, gains, news, made, sums, sems = refs[base + 5 :]
        copies = Copies(sems)
        first = [
            copies.start(residual_ref.at[:, there], old),
            copies.start(gain_ref.at[:, there], gains),
        ]
        if so_far:
            first.append(copies.start(refs[18], sums))
        else:
            sums[...] = jnp.zeros_like(sums)
        loads, slots = [], []
        for k, part in enumerate(stream.parts):
            blocks = pair_sum(at, x, r, 0, part, 0, 0, 0)
            blocks = blocks + [v[k].at[0], w[k].at[0], u[k]]
            slots.append([taken.at[k, j, :, pl.ds(0, part.features)] for j in range(5)])
            loads.append([copies.start(b, s) for b, s in zip(blocks, slots[k])])
        for copy in first:
            copy.wait()
        total = sums[...]
        storing = []
        for k, part in enumerate(stream.parts):
            for copy in loads[k]:
                copy.wait()

            def body(columns, carry, k=k, offset=part.start - stream.start):
                here = pl.ds(pl.multiple_of(offset + columns.start, 128), STEP)
                x = total_of(slots[k], columns) + old[:, here].astype(jnp.float32)
                news[:, here] = bf16(x)
                made[k, :, columns] = bf16(x * gains[:, here])
                square = x * x
                return carry + square[:, :128] + square[:, 128:]

            total = by_columns(part.features, body)(total)
            if not part.note:
                here = made.at[k, :, pl.ds(0, part.features)]
                storing.append(copies.start(here, gained_out[k].at[:, stream.place_of(k)]))
        sums[...] = total
        storing.append(copies.start(news, stream_out.at[:, there]))
        storing.append(copies.start(sums, squares_out))
        for k, part in enumerate(stream.parts):
            if part.note:
                mean = jnp.sum(total, axis=1, keepdims=True) / D
                scale = jnp.broadcast_to(lax.rsqrt(mean + 1e-05), (ROWS, NOTE))
                high = bf16(scale).astype(jnp.float32)
                middle = bf16(scale - high).astype(jnp.float32)
                low = scale - high - middle
                lane = lax.broadcasted_iota(jnp.int32, (ROWS, NOTE), 1)
                parts = jnp.where(lane == 0, high, jnp.where(lane == 1, middle, low))
                made[k, :, pl.ds(part.features, NOTE)] = bf16(jnp.where(lane < 3, parts, 0.0))
                here = made.at[k, :, pl.ds(0, part.sent)]
                storing.append(copies.start(here, gained_out[k].at[:, stream.place_of(k)]))
        for copy in storing:
            copy.wait()

    outs = [shape(ROWS, D)]
    outs += [shape(ROWS, w) for w in WIDTHS]
    outs += [shape(ROWS, 128, dtype=jnp.float32)]
    scratch = [
        pltpu.VMEM((3, 5, ROWS, widest), jnp.bfloat16),
        pltpu.VMEM((ROWS, stream.features), jnp.bfloat16),
        pltpu.VMEM((1, stream.features), jnp.float32),
        pltpu.VMEM((ROWS, stream.features), jnp.bfloat16),
        pltpu.VMEM((3, ROWS, widest + NOTE), jnp.bfloat16),
        pltpu.VMEM((ROWS, 128), jnp.float32),
    ]
    aliases = {14: 0, 15: 1, 16: 2, 17: 3} if so_far else {}
    out = call("finish", kernel, ins, outs, scratch, 3 * 5 + 8, after, aliases)
    return out


def four_blocks(place, held, stream, after):
    def items(at, refs):
        found = []
        for k, part in enumerate(stream.parts):
            for e in range(4):
                source = refs[e * 3 + k].at[:, stream.place_of(k)]
                found.append((k, e, source))
                found.append((3, (e, slice(None), stream.sent(part)), source))
        return found

    outs = [shape(4, ROWS, part.sent) for part in stream.parts]
    outs.append(shape(4, ROWS, stream.features + stream.note))
    out = copied("four", [place, *held], outs, items, after)
    return out[:3], out[3]


def multiplied(place, side, own, other, weight, total, stream, notes, after):
    last = bool(notes)
    half = NZ * NY * ROWS
    ins = [*own, *other, *notes]
    n = len(ins)
    more = [] if total is None else [total]

    def position(part, e1, e2, e3, c):
        z, y = part.apart(e1, e2, e3)
        return pl.ds((c * NZ * NY + z * NY + y) * ROWS, ROWS)

    def kernel(place_ref, *refs):
        weight_ref = refs[n]
        total_ref = None if total is None else refs[n + 1]
        at = n + 1 + len(more) + len(after)
        target = refs[at]
        rows, held, sems = refs[at + 1], refs[at + 2], refs[-1]
        out = refs[at + 3] if last else target
        copies = Copies(sems)
        loads = []
        for k, part in enumerate(stream.parts):
            columns = stream.sent(part)
            there = pl.ds(part.start, part.features)
            here = pl.ds(part.start - stream.start, part.features)
            going = [copies.start(weight_ref.at[there], held.at[here])]
            for e in range(4):
                to = rows.at[pl.ds(e * ROWS, ROWS), columns]
                going.append(copies.start(refs[k].at[e], to))
                source = refs[3 + k].at[e] if len(other) > 1 else refs[3].at[e, :, columns]
                to = rows.at[pl.ds((4 + e) * ROWS, ROWS), columns]
                going.append(copies.start(source, to))
            loads.append(going)
        if last:
            part = stream.parts[2]
            near, beside, notes_held = refs[n - 2], refs[n - 1], refs[at + 4]
            first = [
                copies.start(near.at[:, :, pl.ds(part.features, NOTE)], notes_held.at[0]),
                copies.start(beside.at[:, :, pl.ds(stream.features, NOTE)], notes_held.at[1]),
            ]
        if total_ref is None:
            out[...] = jnp.zeros_like(out)
        else:
            out[...] = total_ref[...]
        for k, part in enumerate(stream.parts):
            for copy in loads[k]:
                copy.wait()
            here = pl.ds(part.start - stream.start, part.features)
            product = jnp.dot(rows[:, here], held[here, :], preferred_element_type=jnp.float32)
            for c in range(NC):
                for e in range(4):
                    some = (c * 4 + e) * ROWS
                    out[position(part, side, e // 2, e % 2, c), :] += product[some : some + ROWS]
        if last:
            for copy in first:
                copy.wait()
            part = stream.parts[2]
            for e1 in range(2):
                for e in range(4):
                    for c in range(NC):
                        if e1 == side:
                            some = pl.ds((c * 4 + e) * ROWS, ROWS)
                            note = rows[some, pl.ds(stream.features, NOTE)]
                        else:
                            note = notes_held[c, e]
                        scale = jnp.sum(note.astype(jnp.float32), axis=1, keepdims=True)
                        apart = part.apart(e1, e // 2, e % 2)
                        to = row_block(place_ref, apart) * NC + lax.bitwise_xor(place_ref[2], c)
                        to = pl.ds(pl.multiple_of(to * ROWS, ROWS), ROWS)
                        here = position(part, e1, e // 2, e % 2, c)
                        target[to, :] = bf16(out[here, :] * scale)

    scratch = [
        pltpu.VMEM((half, stream.features + stream.note), jnp.bfloat16),
        pltpu.VMEM((stream.features, COLS), jnp.bfloat16),
    ]
    if last:
        scratch.append(pltpu.VMEM((2 * half, COLS), jnp.float32))
        scratch.append(pltpu.VMEM((NC, 4, ROWS, NOTE), jnp.bfloat16))
    dtype = jnp.bfloat16 if last else jnp.float32
    return pl.pallas_call(
        kernel,
        in_specs=[SMEM] + [ANY] * (n + 1) + [VMEM] * len(more) + [ANY] * len(after),
        name="multiply",
        out_specs=VMEM,
        out_shape=shape(2 * half, COLS, dtype=dtype),
        scratch_shapes=scratch + [pltpu.SemaphoreType.DMA((29,))],
        compiler_params=pltpu.CompilerParams(vmem_limit_bytes=PRODUCT_BYTES),
        cost_estimate=pl.CostEstimate(flops=0, bytes_accessed=1024, transcendentals=0),
    )(place, *ins, weight, *more, *after)


ORDERS = (("a", "b", "z"), ("b", "z", "a"), ("z", "a", "b"))


def stream_of(start, sizes, note, before):
    parts = []
    for i, (size, dims) in enumerate(zip(sizes, ORDERS)):
        parts.append(Part(start, size, dims, note if i == len(sizes) - 1 else 0))
        start += size
    return Stream(parts, before)


FIRST = stream_of(0, (3072, 3072, 3072), 0, (0, 0, 0))
SECOND = stream_of(9216, (2304, 2304, 2560), NOTE, (3072, 3072, 3072))
WIDTHS = [a.sent + b.sent for a, b in zip(FIRST.parts, SECOND.parts)]


def per_device(partials, residual, norm_gain, qkv_weight):
    t = lax.axis_index("tensor")
    core, y, z = t % 2, (t // 2) % 4, t // 8
    place = jnp.stack([z, y, core]).astype(jnp.int32)
    terms = partials.reshape(NZ * NY * NC, ROWS, D)
    gain = norm_gain.astype(jnp.float32).reshape(1, D)

    def along(step, arrays):
        return [send(x, TO[ORDERS[k][step]]) for k, x in enumerate(arrays)]

    def across(arrays):
        return [send(x, TO_CORE) for x in arrays]

    a, b = FIRST, SECOND
    a_give = give(place, terms, [(a, 1)], [])
    a_got = across(a_give)[0]
    give_rest = give(place, terms, [(a, 0), (b, 0), (b, 1)], [a_give[0]])
    give_rest, _ = lax.optimization_barrier((give_rest[0], a_got))
    rest = send(give_rest, TO_CORE)
    a_out = first_step(place, terms, a_got, 0, a, [give_rest])
    a_one = along(0, a_out)
    b_out = first_step(place, terms, rest, D - b.start, b, [a_out[0]])
    b_one = along(0, b_out)
    a_out = second_step(place, terms, rest, a_one, a, [b_out[0]])
    a_two = along(1, a_out)
    b_out = second_step(place, terms, rest, b_one, b, [a_out[0]])
    b_two = along(1, b_out)
    a_out = third_step(place, terms, rest, a_one, a_two, a, [b_out[0]])
    a_three = along(2, a_out)
    b_out = third_step(place, terms, rest, b_one, b_two, b, [a_out[0]])
    b_three = along(2, b_out)
    so_far = finish(
        place, terms, rest, a_one, a_two, a_three, a, residual, gain, (), [b_out[0]]
    )
    stream, *rows, _ = finish(
        place, terms, rest, b_one, b_two, b_three, b, residual, gain, so_far, []
    )
    rows_z = along(2, rows)
    rows_y = along(1, rows)
    rows_zy = along(1, rows_z)
    held = [*rows, *rows_z, *rows_y, *rows_zy]
    a_near, a_beside = four_blocks(place, held, a, [])
    a_far = along(0, a_near)
    a_beside = send(a_beside, TO_CORE)
    b_near, b_beside = four_blocks(place, held, b, [a_near[0]])
    b_far = along(0, b_near)
    b_beside = send(b_beside, TO_CORE)

    near = functools.partial(multiplied, place, 0)
    far = functools.partial(multiplied, place, 1)
    total = near(a_near, [a_beside], qkv_weight, None, a, [], [b_near[0]])
    total = near(b_near, [b_beside], qkv_weight, total, b, [], [])
    *a_ready, _ = lax.optimization_barrier((*a_far, total))
    total = far(a_far, across(a_ready), qkv_weight, total, a, [], [])
    *b_ready, _ = lax.optimization_barrier((*b_far, total))
    notes = [b_near[2], b_beside]
    projected = far(b_far, across(b_ready), qkv_weight, total, b, notes, [])
    return stream, projected


def solution(mesh):
    in_specs = (P("tensor", "dp", None), P(("dp", "tensor"), None), P(), P(None, "tensor"))
    out_specs = (P(("dp", "tensor"), None), P("dp", "tensor"))
    return jax.shard_map(
        per_device, mesh=mesh, in_specs=in_specs, out_specs=out_specs, check_vma=False
    )
```

```python
import functools

import jax
import jax.numpy as jnp
from jax import lax
from jax.experimental import pallas as pl
from jax.experimental.pallas import tpu as pltpu
from jax.sharding import PartitionSpec as P

NZ, NY, NC = 2, 4, 2
ROWS = 32
D = 16384
COLS = 640
NOTE = 128
ANY = pl.BlockSpec(memory_space=pl.ANY)
VMEM = pl.BlockSpec(memory_space=pltpu.VMEM)
MIB = 1024 * 1024
SUM_BYTES = 45 * MIB
ROW_BYTES = 16 * MIB
PRODUCT_BYTES = 41 * MIB


def index_of(z, y, c):
    return (z * NY + y % NY) * NC + c


def pairs(move):
    return [
        (index_of(z, y, c), index_of(*move(z, y, c)))
        for z in range(NZ)
        for y in range(NY)
        for c in range(NC)
    ]


MOVES = {"a": (0, 1), "b": (0, 3), "z": (1, 0)}
TO = {d: pairs(lambda z, y, c, m=m: (z ^ m[0], y ^ m[1], c)) for d, m in MOVES.items()}
TO_CORE = pairs(lambda z, y, c: (z, y, 1 - c))


def send(x, where):
    return lax.ppermute(x, "tensor", where)


def bf16(x):
    return x.astype(jnp.bfloat16)


def shape(*dims, dtype=jnp.bfloat16):
    return jax.ShapeDtypeStruct(dims, dtype)


class Copies:
    def __init__(self, sems):
        self.sems, self.count = sems, 0

    def start(self, source, target):
        copy = pltpu.make_async_copy(source, target, self.sems.at[self.count])
        self.count += 1
        copy.start()
        return copy


def by_columns(width, body):
    step = 512 if width % 512 == 0 else 256

    def at(i, carry):
        return body(pl.ds(pl.multiple_of(i * step, step), step), carry)

    return functools.partial(lax.fori_loop, 0, width // step, at)


def total_of(sources, columns):
    total = sources[0][:, columns].astype(jnp.float32)
    for ref in sources[1:]:
        total = total + ref[:, columns].astype(jnp.float32)
    return total


def where_am_i():
    t = lax.axis_index("tensor")
    return t // (NY * NC), t // NC % NY, t % NC


def call(name, kernel, ins, outs, scratch, copies, after, aliases={}, limit=SUM_BYTES):
    return pl.pallas_call(
        lambda *refs: kernel(where_am_i(), *refs),
        in_specs=[ANY] * (len(ins) - 1 + len(after)),
        out_specs=[ANY] * len(outs),
        name=name,
        out_shape=outs,
        scratch_shapes=scratch + [pltpu.SemaphoreType.DMA((copies,))],
        input_output_aliases=aliases,
        compiler_params=pltpu.CompilerParams(vmem_limit_bytes=limit),
        cost_estimate=pl.CostEstimate(flops=0, bytes_accessed=1024, transcendentals=0),
    )(*ins[1:], *after)


def copied(name, ins, outs, items, after):
    n = len(ins)

    def kernel(*refs):
        place, sources = refs[0], refs[1:n]
        targets, sems = refs[n + len(after) : -1], refs[-1]
        copies = Copies(sems)
        going = [
            copies.start(source, targets[k].at[index])
            for k, index, source in items(place, sources)
        ]
        for copy in going:
            copy.wait()

    return call(name, kernel, ins, outs, [], 36, after, limit=ROW_BYTES)


def added(name, ins, steps, others, stream, after):
    n, count = len(ins), len(steps)
    most = 1 + len(others([None] * n, 0))
    widest = max(part.features for part in stream.parts)

    def kernel(*refs):
        at, x, targets = refs[0], refs[1], refs[n + len(after) : n + len(after) + 3]
        taken, made, sems = refs[-3:]
        copies = Copies(sems)
        loads, storing = [], []
        for k, part in enumerate(stream.parts):
            inside = pl.ds(0, part.features)
            going = []
            for e, step in enumerate(steps):
                source = x.at[block(at, part.apart(*step), 0), :, part.columns]
                going.append(copies.start(source, taken.at[0, k, e, :, inside]))
            for j, source in enumerate(others(refs, k)):
                going.append(copies.start(source, taken.at[1 + j, k, :, :, inside]))
            loads.append(going)
        for k, part in enumerate(stream.parts):
            for copy in loads[k]:
                copy.wait()

            def one(e, carry, k=k, width=part.features):
                def body(columns, carry):
                    total = taken[0, k, e, :, columns].astype(jnp.float32)
                    for j in range(1, most):
                        total = total + taken[j, k, e, :, columns].astype(jnp.float32)
                    made[k, e, :, columns] = bf16(total)
                    return carry

                return by_columns(width, body)(carry)

            lax.fori_loop(0, count, one, 0)
            source = made.at[k, :, :, pl.ds(0, part.features)]
            storing.append(copies.start(source, targets[k]))
        for copy in storing:
            copy.wait()

    scratch = [
        pltpu.VMEM((most, 3, count, ROWS, widest), jnp.bfloat16),
        pltpu.VMEM((3, count, ROWS, widest), jnp.bfloat16),
    ]
    outs = [shape(count, ROWS, part.features) for part in stream.parts]
    return call(name, kernel, ins, outs, scratch, 3 * (count + most), after)


class Part:
    def __init__(self, start, features, dims, note=0):
        self.start, self.features, self.note = start, features, note
        self.sent = features + note
        self.columns = pl.ds(start, features)
        self.dims = dims

    def apart(self, *steps):
        z = y = 0
        for d, step in zip(self.dims, steps):
            if step:
                z, y = z ^ MOVES[d][0], y ^ MOVES[d][1]
        return z, y


class Stream:
    def __init__(self, parts, before):
        self.parts, self.before = parts, before
        self.features = sum(p.features for p in parts)
        self.note = sum(p.note for p in parts)
        self.offsets = [sum(p.features for p in parts[:k]) for k in range(len(parts))]

    def local(self, k, extra=False):
        return pl.ds(self.offsets[k], self.parts[k].sent if extra else self.parts[k].features)

    def beside(self, k):
        return pl.ds(sum(WIDTHS[:k]) + self.before[k], self.parts[k].sent)

    def place_of(self, k):
        return pl.ds(self.before[k], self.parts[k].sent)


def row_block(place, apart):
    z, y = place[0], place[1]
    return lax.bitwise_xor(z, apart[0]) * NY + lax.bitwise_xor(y, apart[1])


def block(place, apart, dc):
    c = place[2]
    return row_block(place, apart) * NC + lax.bitwise_xor(c, dc)


def give(place, terms, wanted, width, after):
    def items(at, x):
        return [
            (
                (e2 * 2 + e3, slice(None), pl.ds(position, part.features)),
                x.at[block(at, part.apart(first, e2, e3), 1), :, part.columns],
            )
            for part, first, position in wanted
            for e2 in (1, 0)
            for e3 in (0, 1)
        ]

    def kernel(*refs):
        at, x = refs[:2]
        target, held, sems = refs[-3:]
        copies = Copies(sems)
        todo = []
        for index, source in items(at, x):
            todo.append((index, copies.start(source, held.at[index])))
        storing = []
        for index, copy in todo:
            copy.wait()
            storing.append(copies.start(held.at[index], target.at[index]))
        for copy in storing:
            copy.wait()

    scratch = [pltpu.VMEM((4, ROWS, width), jnp.bfloat16)]
    out = shape(4, ROWS, width)
    return call("give", kernel, [place, terms], [out], scratch, 8 * len(wanted), after)


def from_core(ref, blocks, position, part):
    if ref is None:
        return None
    return ref.at[blocks, :, pl.ds(position, part.features)]


def pick(ref, index):
    return None if ref is None else ref.at[index]


QUARTERS = ((0, 0), (0, 1), (1, 0), (1, 1))


def first_step(place, terms, got, offset, stream, after):
    def others(refs, k):
        return [from_core(refs[2], pl.ds(0, 4), offset + stream.offsets[k], stream.parts[k])]

    steps = [(1, *q) for q in QUARTERS]
    return added("first", [place, terms, got], steps, others, stream, after)


def second_step(place, terms, rest, one, stream, after):
    def others(refs, k):
        some = pl.ds(2, 2)
        return [from_core(refs[2], some, stream.parts[k].start, stream.parts[k]), pick(refs[3 + k], some)]

    steps = [(0, 1, 0), (0, 1, 1)]
    return added("second", [place, terms, rest, *one], steps, others, stream, after)


def third_step(place, terms, rest, one, two, stream, after):
    def others(refs, k):
        some = pl.ds(1, 1)
        got = from_core(refs[2], some, stream.parts[k].start, stream.parts[k])
        return [got, pick(refs[3 + k], some), pick(refs[6 + k], some)]

    steps = [(0, 0, 1)]
    return added("third", [place, terms, rest, *one, *two], steps, others, stream, after)


def finish(place, terms, rest, one, two, three, stream, residual, gain, so_far, after):
    ins = [place, terms, rest, *one, *two, *three, residual, gain, *so_far]
    widest = max(part.features for part in stream.parts)

    def kernel(*refs):
        at, x = refs[0], refs[1]
        r, v, w, u = refs[2], refs[3:6], refs[6:9], refs[9:12]
        residual_ref, gain_ref = refs[12:14]
        base = len(ins) + len(after)
        stream_out, gained_out, squares_out = refs[base], refs[base + 1 : base + 4], refs[base + 4]
        taken, old, gains, news, made, sums, sems = refs[base + 5 :]
        copies = Copies(sems)
        first = []
        for k, part in enumerate(stream.parts):
            here = stream.local(k)
            first.append(copies.start(residual_ref.at[:, part.columns], old.at[:, here]))
            first.append(copies.start(gain_ref.at[:, part.columns], gains.at[:, here]))
        if so_far:
            first.append(copies.start(refs[18], sums))
        else:
            sums[...] = jnp.zeros_like(sums)
        loads, slots = [], []
        for k, part in enumerate(stream.parts):
            mine = x.at[block(at, part.apart(0, 0, 0), 0), :, part.columns]
            blocks = [mine, from_core(r, 0, part.start, part), v[k].at[0], w[k].at[0], u[k].at[0]]
            slots.append([taken.at[k, j, :, pl.ds(0, part.features)] for j in range(5)])
            loads.append([copies.start(b, s) for b, s in zip(blocks, slots[k])])
        for copy in first:
            copy.wait()
        total = sums[...]
        storing = []
        for k, part in enumerate(stream.parts):
            for copy in loads[k]:
                copy.wait()

            def body(columns, carry, k=k, offset=stream.offsets[k]):
                here = pl.ds(pl.multiple_of(offset + columns.start, 128), columns.size)
                x = total_of(slots[k], columns) + old[:, here].astype(jnp.float32)
                news[:, here] = bf16(x)
                made[k, :, columns] = bf16(x * gains[:, here])
                square = x * x
                return carry + sum(square[:, i : i + 128] for i in range(0, columns.size, 128))

            total = by_columns(part.features, body)(total)
            here = news.at[:, stream.local(k)]
            storing.append(copies.start(here, stream_out.at[:, part.columns]))
            if not part.note:
                here = made.at[k, :, pl.ds(0, part.features)]
                storing.append(copies.start(here, gained_out[k].at[:, stream.place_of(k)]))
        sums[...] = total
        storing.append(copies.start(sums, squares_out))
        for k, part in enumerate(stream.parts):
            if part.note:
                mean = jnp.sum(total, axis=1, keepdims=True) / D
                scale = jnp.broadcast_to(lax.rsqrt(mean + 1e-05), (ROWS, NOTE))
                high = bf16(scale).astype(jnp.float32)
                middle = bf16(scale - high).astype(jnp.float32)
                low = scale - high - middle
                lane = lax.broadcasted_iota(jnp.int32, (ROWS, NOTE), 1)
                parts = jnp.where(lane == 0, high, jnp.where(lane == 1, middle, low))
                made[k, :, pl.ds(part.features, NOTE)] = bf16(jnp.where(lane < 3, parts, 0.0))
                here = made.at[k, :, pl.ds(0, part.sent)]
                storing.append(copies.start(here, gained_out[k].at[:, stream.place_of(k)]))
        for copy in storing:
            copy.wait()

    outs = [shape(ROWS, D)]
    outs += [shape(ROWS, w) for w in WIDTHS]
    outs += [shape(ROWS, 128, dtype=jnp.float32)]
    scratch = [
        pltpu.VMEM((3, 5, ROWS, widest), jnp.bfloat16),
        pltpu.VMEM((ROWS, stream.features), jnp.bfloat16),
        pltpu.VMEM((1, stream.features), jnp.float32),
        pltpu.VMEM((ROWS, stream.features), jnp.bfloat16),
        pltpu.VMEM((3, ROWS, widest + NOTE), jnp.bfloat16),
        pltpu.VMEM((ROWS, 128), jnp.float32),
    ]
    aliases = {13: 0, 14: 1, 15: 2, 16: 3} if so_far else {}
    out = call("finish", kernel, ins, outs, scratch, 3 * 5 + 14, after, aliases)
    return out


def four_blocks(place, held, after):
    def items(at, refs):
        found = []
        for i, stream in enumerate((ONE, TWO)):
            for k in range(3):
                for e in range(4):
                    found.append((3 * i + k, e, refs[e * 3 + k].at[:, stream.place_of(k)]))
        for k in range(3):
            for e in range(4):
                to = pl.ds(sum(WIDTHS[:k]), WIDTHS[k])
                found.append((6, (e, slice(None), to), refs[e * 3 + k]))
        return found

    outs = [shape(4, ROWS, part.sent) for s in (ONE, TWO) for part in s.parts]
    outs.append(shape(4, ROWS, sum(WIDTHS)))
    out = copied("four", [place, *held], outs, items, after)
    return out[:3], out[3:6], out[6]


def multiplied(place, side, own, other, weight, total, stream, notes, after):
    last = bool(notes)
    half = NZ * NY * ROWS
    ins = [*own, *other, *notes]
    n = len(ins)
    more = [] if total is None else [total]

    def position(part, e1, e2, e3, c):
        z, y = part.apart(e1, e2, e3)
        return pl.ds((c * NZ * NY + z * NY + y) * ROWS, ROWS)

    def kernel(*refs):
        weight_ref = refs[n]
        at = n + 1 + len(more) + len(after)
        target = refs[at]
        rows, held, out, sems = refs[at + 1], refs[at + 2], refs[at + 3], refs[-1]
        copies = Copies(sems)
        loads = []
        for k, part in enumerate(stream.parts):
            columns = stream.local(k, True)
            half_depth = part.features // 2
            going = []
            for h in range(2):
                there = pl.ds(part.start + h * half_depth, half_depth)
                here = pl.ds(stream.offsets[k] + h * half_depth, half_depth)
                going.append(copies.start(weight_ref.at[there], held.at[here]))
            for e in range(4):
                to = rows.at[pl.ds(e * ROWS, ROWS), columns]
                going.append(copies.start(refs[k].at[e], to))
                source = refs[3 + k].at[e] if len(other) > 1 else refs[3].at[e, :, stream.beside(k)]
                to = rows.at[pl.ds((4 + e) * ROWS, ROWS), columns]
                going.append(copies.start(source, to))
            loads.append(going)
        if last:
            part = stream.parts[2]
            near, beside, notes_held = refs[n - 2], refs[n - 1], refs[at + 4]
            first = [
                copies.start(near.at[:, :, pl.ds(part.features, NOTE)], notes_held.at[0]),
                copies.start(beside.at[:, :, pl.ds(sum(WIDTHS) - NOTE, NOTE)], notes_held.at[1]),
            ]
        if more:
            before = copies.start(refs[n + 1], out)
        else:
            out[...] = jnp.zeros_like(out)
        for k, part in enumerate(stream.parts):
            half_depth = part.features // 2
            start = stream.offsets[k]
            for copy in [loads[k][0], *loads[k][2:]]:
                copy.wait()
            here = pl.ds(start, half_depth)
            product = jnp.dot(rows[:, here], held[here, :], preferred_element_type=jnp.float32)
            loads[k][1].wait()
            here = pl.ds(start + half_depth, half_depth)
            product += jnp.dot(rows[:, here], held[here, :], preferred_element_type=jnp.float32)
            if more and k == 0:
                before.wait()
            for c in range(NC):
                for e in range(4):
                    some = (c * 4 + e) * ROWS
                    out[position(part, side, e // 2, e % 2, c), :] += product[some : some + ROWS]
        if not last:
            copies.start(out, target).wait()
        else:
            for copy in first:
                copy.wait()
            part, place_now = stream.parts[2], where_am_i()
            for e1 in range(2):
                for e in range(4):
                    for c in range(NC):
                        if e1 == side:
                            some = pl.ds((c * 4 + e) * ROWS, ROWS)
                            note = rows[some, pl.ds(stream.features, NOTE)]
                        else:
                            note = notes_held[c, e]
                        scale = jnp.sum(note.astype(jnp.float32), axis=1, keepdims=True)
                        apart = part.apart(e1, e // 2, e % 2)
                        to = row_block(place_now, apart) * NC + lax.bitwise_xor(place_now[2], c)
                        to = pl.ds(pl.multiple_of(to * ROWS, ROWS), ROWS)
                        here = position(part, e1, e // 2, e % 2, c)
                        target[to, :] = bf16(out[here, :] * scale)

    scratch = [
        pltpu.VMEM((half, stream.features + stream.note), jnp.bfloat16),
        pltpu.VMEM((stream.features, COLS), jnp.bfloat16),
    ]
    scratch.append(pltpu.VMEM((2 * half, COLS), jnp.float32))
    if last:
        scratch.append(pltpu.VMEM((NC, 4, ROWS, NOTE), jnp.bfloat16))
    dtype = jnp.bfloat16 if last else jnp.float32
    return pl.pallas_call(
        kernel,
        in_specs=[ANY] * (n + 1 + len(more) + len(after)),
        name="multiply",
        out_specs=VMEM if last else ANY,
        out_shape=shape(2 * half, COLS, dtype=dtype),
        scratch_shapes=scratch + [pltpu.SemaphoreType.DMA((34,))],
        compiler_params=pltpu.CompilerParams(vmem_limit_bytes=PRODUCT_BYTES),
        cost_estimate=pl.CostEstimate(flops=0, bytes_accessed=1024, transcendentals=0),
    )(*ins, weight, *more, *after)


ORDERS = (("a", "b", "z"), ("b", "z", "a"), ("z", "a", "b"))


def streams_of(first, second, note):
    runs, start = ([], []), 0
    for k, dims in enumerate(ORDERS):
        runs[0].append(Part(start, first[k], dims))
        runs[1].append(Part(start + first[k], second[k], dims, note if k == 2 else 0))
        start += first[k] + second[k]
    return Stream(runs[0], (0, 0, 0)), Stream(runs[1], first)


FIRST, SECOND = streams_of((2560, 4096, 4096), (3072, 1024, 1536), NOTE)
ONE, TWO = streams_of((4096, 4096, 4096), (1536, 1024, 1536), NOTE)
WIDTHS = [a.sent + b.sent for a, b in zip(FIRST.parts, SECOND.parts)]


def per_device(partials, residual, norm_gain, qkv_weight):
    place = None
    terms = partials.reshape(NZ * NY * NC, ROWS, D)
    gain = norm_gain.astype(jnp.float32).reshape(1, D)

    def along(step, arrays):
        return [send(x, TO[ORDERS[k][step]]) for k, x in enumerate(arrays)]

    def across(arrays):
        return [send(x, TO_CORE) for x in arrays]

    a, b = FIRST, SECOND
    wanted = [(part, 1, a.offsets[k]) for k, part in enumerate(a.parts)]
    a_give = give(place, terms, wanted, a.features, [])
    a_got = across(a_give)[0]
    wanted = [(part, 0, part.start) for part in (*a.parts, *b.parts)]
    wanted += [(part, 1, D + b.offsets[k]) for k, part in enumerate(b.parts)]
    give_rest = give(place, terms, wanted, D + b.features, [a_give[0]])
    give_rest, _ = lax.optimization_barrier((give_rest[0], a_got))
    rest = send(give_rest, TO_CORE)
    a_out = first_step(place, terms, a_got, 0, a, [give_rest])
    a_one = along(0, a_out)
    b_out = first_step(place, terms, rest, D, b, [a_out[0]])
    b_one = along(0, b_out)
    a_out = second_step(place, terms, rest, a_one, a, [b_out[0]])
    a_two = along(1, a_out)
    b_out = second_step(place, terms, rest, b_one, b, [a_out[0]])
    b_two = along(1, b_out)
    a_out = third_step(place, terms, rest, a_one, a_two, a, [b_out[0]])
    a_three = along(2, a_out)
    b_out = third_step(place, terms, rest, b_one, b_two, b, [a_out[0]])
    b_three = along(2, b_out)
    so_far = finish(
        place, terms, rest, a_one, a_two, a_three, a, residual, gain, (), [b_out[0]]
    )
    stream, *rows, _ = finish(
        place, terms, rest, b_one, b_two, b_three, b, residual, gain, so_far, []
    )
    rows_z = along(2, rows)
    rows_y = along(1, rows)
    rows_zy = along(1, rows_z)
    held = [*rows, *rows_z, *rows_y, *rows_zy]
    a_near, b_near, beside = four_blocks(place, held, [])
    a_far = along(0, a_near)
    b_far = along(0, b_near)
    beside = send(beside, TO_CORE)

    near = functools.partial(multiplied, place, 0)
    far = functools.partial(multiplied, place, 1)
    total = near(a_near, [beside], qkv_weight, None, ONE, [], [])
    total = near(b_near, [beside], qkv_weight, total, TWO, [], [])
    *a_ready, _ = lax.optimization_barrier((*a_far, total))
    total = far(a_far, across(a_ready), qkv_weight, total, ONE, [], [])
    *b_ready, _ = lax.optimization_barrier((*b_far, total))
    notes = [b_near[2], beside]
    projected = far(b_far, across(b_ready), qkv_weight, total, TWO, notes, [])
    return stream, projected


def solution(mesh):
    in_specs = (P("tensor", "dp", None), P(("dp", "tensor"), None), P(), P(None, "tensor"))
    out_specs = (P(("dp", "tensor"), None), P("dp", "tensor"))
    return jax.shard_map(
        per_device, mesh=mesh, in_specs=in_specs, out_specs=out_specs, check_vma=False
    )
```

```python
import functools

import jax
import jax.numpy as jnp
from jax import lax
from jax.experimental import pallas as pl
from jax.experimental.pallas import tpu as pltpu
from jax.sharding import PartitionSpec as P

NZ, NY, NC = 2, 4, 2
ROWS = 32
D = 16384
COLS = 640
NOTE = 128
ANY = pl.BlockSpec(memory_space=pl.ANY)
VMEM = pl.BlockSpec(memory_space=pltpu.VMEM)
MIB = 1024 * 1024
SUM_BYTES = 45 * MIB
ROW_BYTES = 16 * MIB
PRODUCT_BYTES = 41 * MIB


def index_of(z, y, c):
    return (z * NY + y % NY) * NC + c


def pairs(move):
    return [
        (index_of(z, y, c), index_of(*move(z, y, c)))
        for z in range(NZ)
        for y in range(NY)
        for c in range(NC)
    ]


MOVES = {"a": (0, 1), "b": (0, 3), "z": (1, 0)}
TO = {d: pairs(lambda z, y, c, m=m: (z ^ m[0], y ^ m[1], c)) for d, m in MOVES.items()}
TO_CORE = pairs(lambda z, y, c: (z, y, 1 - c))


def send(x, where):
    return lax.ppermute(x, "tensor", where)


def bf16(x):
    return x.astype(jnp.bfloat16)


def shape(*dims, dtype=jnp.bfloat16):
    return jax.ShapeDtypeStruct(dims, dtype)


class Copies:
    def __init__(self, sems):
        self.sems, self.count = sems, 0

    def start(self, source, target):
        copy = pltpu.make_async_copy(source, target, self.sems.at[self.count])
        self.count += 1
        copy.start()
        return copy


def by_columns(width, body):
    step = 512 if width % 512 == 0 else 256

    def at(i, carry):
        return body(pl.ds(pl.multiple_of(i * step, step), step), carry)

    steps = width // step
    unroll = next(u for u in (3, 7, 5, 2, 1) if steps % u == 0)
    return functools.partial(lax.fori_loop, 0, steps, at, unroll=unroll)


def total_of(sources, columns):
    total = sources[0][:, columns].astype(jnp.float32)
    for ref in sources[1:]:
        total = total + ref[:, columns].astype(jnp.float32)
    return total


def where_am_i():
    t = lax.axis_index("tensor")
    return t // (NY * NC), t // NC % NY, t % NC


def call(name, kernel, ins, outs, scratch, copies, after, aliases={}, limit=SUM_BYTES):
    return pl.pallas_call(
        lambda *refs: kernel(where_am_i(), *refs),
        in_specs=[ANY] * (len(ins) - 1 + len(after)),
        out_specs=[ANY] * len(outs),
        name=name,
        out_shape=outs,
        scratch_shapes=scratch + [pltpu.SemaphoreType.DMA((copies,))],
        input_output_aliases=aliases,
        compiler_params=pltpu.CompilerParams(vmem_limit_bytes=limit),
        cost_estimate=pl.CostEstimate(flops=0, bytes_accessed=1024, transcendentals=0),
    )(*ins[1:], *after)


def copied(name, ins, outs, items, after):
    n = len(ins)

    def kernel(*refs):
        place, sources = refs[0], refs[1:n]
        targets, sems = refs[n + len(after) : -1], refs[-1]
        copies = Copies(sems)
        going = [
            copies.start(source, targets[k].at[index])
            for k, index, source in items(place, sources)
        ]
        for copy in going:
            copy.wait()

    return call(name, kernel, ins, outs, [], 36, after, limit=ROW_BYTES)


def added(name, ins, steps, others, stream, after):
    n, count = len(ins), len(steps)
    most = 1 + len(others([None] * n, 0))
    widest = max(part.features for part in stream.parts)

    def kernel(*refs):
        at, x, targets = refs[0], refs[1], refs[n + len(after) : n + len(after) + 3]
        taken, made, sems = refs[-3:]
        copies = Copies(sems)
        loads, storing = [], []
        for k, part in enumerate(stream.parts):
            inside = pl.ds(0, part.features)
            going = []
            for e, step in enumerate(steps):
                source = x.at[block(at, part.apart(*step), 0), :, part.columns]
                going.append(copies.start(source, taken.at[0, k, e, :, inside]))
            for j, source in enumerate(others(refs, k)):
                going.append(copies.start(source, taken.at[1 + j, k, :, :, inside]))
            loads.append(going)
        for k, part in enumerate(stream.parts):
            for copy in loads[k]:
                copy.wait()

            def one(e, carry, k=k, width=part.features):
                def body(columns, carry):
                    total = taken[0, k, e, :, columns].astype(jnp.float32)
                    for j in range(1, most):
                        total = total + taken[j, k, e, :, columns].astype(jnp.float32)
                    made[k, e, :, columns] = bf16(total)
                    return carry

                return by_columns(width, body)(carry)

            lax.fori_loop(0, count, one, 0)
            source = made.at[k, :, :, pl.ds(0, part.features)]
            storing.append(copies.start(source, targets[k]))
        for copy in storing:
            copy.wait()

    scratch = [
        pltpu.VMEM((most, 3, count, ROWS, widest), jnp.bfloat16),
        pltpu.VMEM((3, count, ROWS, widest), jnp.bfloat16),
    ]
    outs = [shape(count, ROWS, part.features) for part in stream.parts]
    return call(name, kernel, ins, outs, scratch, 3 * (count + most), after)


class Part:
    def __init__(self, start, features, dims, note=0):
        self.start, self.features, self.note = start, features, note
        self.sent = features + note
        self.columns = pl.ds(start, features)
        self.dims = dims

    def apart(self, *steps):
        z = y = 0
        for d, step in zip(self.dims, steps):
            if step:
                z, y = z ^ MOVES[d][0], y ^ MOVES[d][1]
        return z, y


class Stream:
    def __init__(self, parts, before):
        self.parts, self.before = parts, before
        self.features = sum(p.features for p in parts)
        self.note = sum(p.note for p in parts)
        self.offsets = [sum(p.features for p in parts[:k]) for k in range(len(parts))]

    def local(self, k, extra=False):
        return pl.ds(self.offsets[k], self.parts[k].sent if extra else self.parts[k].features)

    def beside(self, k):
        return pl.ds(sum(WIDTHS[:k]) + self.before[k], self.parts[k].sent)

    def place_of(self, k):
        return pl.ds(self.before[k], self.parts[k].sent)


def row_block(place, apart):
    z, y = place[0], place[1]
    return lax.bitwise_xor(z, apart[0]) * NY + lax.bitwise_xor(y, apart[1])


def block(place, apart, dc):
    c = place[2]
    return row_block(place, apart) * NC + lax.bitwise_xor(c, dc)


def give(place, terms, wanted, width, after):
    def items(at, x):
        return [
            (
                (e2 * 2 + e3, slice(None), pl.ds(position, part.features)),
                x.at[block(at, part.apart(first, e2, e3), 1), :, part.columns],
            )
            for part, first, position in wanted
            for e2 in (1, 0)
            for e3 in (0, 1)
        ]

    def kernel(*refs):
        at, x = refs[:2]
        target, held, sems = refs[-3:]
        copies = Copies(sems)
        todo = []
        for index, source in items(at, x):
            todo.append((index, copies.start(source, held.at[index])))
        storing = []
        for index, copy in todo:
            copy.wait()
            storing.append(copies.start(held.at[index], target.at[index]))
        for copy in storing:
            copy.wait()

    scratch = [pltpu.VMEM((4, ROWS, width), jnp.bfloat16)]
    out = shape(4, ROWS, width)
    return call("give", kernel, [place, terms], [out], scratch, 8 * len(wanted), after)


def from_core(ref, blocks, position, part):
    if ref is None:
        return None
    return ref.at[blocks, :, pl.ds(position, part.features)]


def pick(ref, index):
    return None if ref is None else ref.at[index]


QUARTERS = ((0, 0), (0, 1), (1, 0), (1, 1))


def first_step(place, terms, got, offset, stream, after):
    def others(refs, k):
        return [from_core(refs[2], pl.ds(0, 4), offset + stream.offsets[k], stream.parts[k])]

    steps = [(1, *q) for q in QUARTERS]
    return added("first", [place, terms, got], steps, others, stream, after)


def second_step(place, terms, rest, one, stream, after):
    def others(refs, k):
        some = pl.ds(2, 2)
        return [from_core(refs[2], some, stream.parts[k].start, stream.parts[k]), pick(refs[3 + k], some)]

    steps = [(0, 1, 0), (0, 1, 1)]
    return added("second", [place, terms, rest, *one], steps, others, stream, after)


def third_step(place, terms, rest, one, two, stream, after):
    def others(refs, k):
        some = pl.ds(1, 1)
        got = from_core(refs[2], some, stream.parts[k].start, stream.parts[k])
        return [got, pick(refs[3 + k], some), pick(refs[6 + k], some)]

    steps = [(0, 0, 1)]
    return added("third", [place, terms, rest, *one, *two], steps, others, stream, after)


def finish(place, terms, rest, one, two, three, stream, residual, gain, so_far, after):
    ins = [place, terms, rest, *one, *two, *three, residual, gain, *so_far]
    widest = max(part.features for part in stream.parts)

    def kernel(*refs):
        at, x = refs[0], refs[1]
        r, v, w, u = refs[2], refs[3:6], refs[6:9], refs[9:12]
        residual_ref, gain_ref = refs[12:14]
        base = len(ins) + len(after)
        stream_out, gained_out, squares_out = refs[base], refs[base + 1 : base + 4], refs[base + 4]
        taken, old, gains, news, made, sums, sems = refs[base + 5 :]
        copies = Copies(sems)
        first = []
        for k, part in enumerate(stream.parts):
            here = stream.local(k)
            first.append(copies.start(residual_ref.at[:, part.columns], old.at[:, here]))
            first.append(copies.start(gain_ref.at[:, part.columns], gains.at[:, here]))
        if so_far:
            first.append(copies.start(refs[18], sums))
        else:
            sums[...] = jnp.zeros_like(sums)
        loads, slots = [], []
        for k, part in enumerate(stream.parts):
            mine = x.at[block(at, part.apart(0, 0, 0), 0), :, part.columns]
            blocks = [mine, from_core(r, 0, part.start, part), v[k].at[0], w[k].at[0], u[k].at[0]]
            slots.append([taken.at[k, j, :, pl.ds(0, part.features)] for j in range(5)])
            loads.append([copies.start(b, s) for b, s in zip(blocks, slots[k])])
        for copy in first:
            copy.wait()
        total = sums[...]
        storing = []
        for k, part in enumerate(stream.parts):
            for copy in loads[k]:
                copy.wait()

            def body(columns, carry, k=k, offset=stream.offsets[k]):
                here = pl.ds(pl.multiple_of(offset + columns.start, 128), columns.size)
                x = total_of(slots[k], columns) + old[:, here].astype(jnp.float32)
                news[:, here] = bf16(x)
                made[k, :, columns] = bf16(x * gains[:, here])
                square = x * x
                return carry + sum(square[:, i : i + 128] for i in range(0, columns.size, 128))

            total = by_columns(part.features, body)(total)
            here = news.at[:, stream.local(k)]
            storing.append(copies.start(here, stream_out.at[:, part.columns]))
            if not part.note:
                here = made.at[k, :, pl.ds(0, part.features)]
                storing.append(copies.start(here, gained_out[k].at[:, stream.place_of(k)]))
        sums[...] = total
        storing.append(copies.start(sums, squares_out))
        for k, part in enumerate(stream.parts):
            if part.note:
                mean = jnp.sum(total, axis=1, keepdims=True) / D
                scale = jnp.broadcast_to(lax.rsqrt(mean + 1e-05), (ROWS, NOTE))
                high = bf16(scale).astype(jnp.float32)
                middle = bf16(scale - high).astype(jnp.float32)
                low = scale - high - middle
                lane = lax.broadcasted_iota(jnp.int32, (ROWS, NOTE), 1)
                parts = jnp.where(lane == 0, high, jnp.where(lane == 1, middle, low))
                made[k, :, pl.ds(part.features, NOTE)] = bf16(jnp.where(lane < 3, parts, 0.0))
                here = made.at[k, :, pl.ds(0, part.sent)]
                storing.append(copies.start(here, gained_out[k].at[:, stream.place_of(k)]))
        for copy in storing:
            copy.wait()

    outs = [shape(ROWS, D)]
    outs += [shape(ROWS, w) for w in WIDTHS]
    outs += [shape(ROWS, 128, dtype=jnp.float32)]
    scratch = [
        pltpu.VMEM((3, 5, ROWS, widest), jnp.bfloat16),
        pltpu.VMEM((ROWS, stream.features), jnp.bfloat16),
        pltpu.VMEM((1, stream.features), jnp.float32),
        pltpu.VMEM((ROWS, stream.features), jnp.bfloat16),
        pltpu.VMEM((3, ROWS, widest + NOTE), jnp.bfloat16),
        pltpu.VMEM((ROWS, 128), jnp.float32),
    ]
    aliases = {13: 0, 14: 1, 15: 2, 16: 3} if so_far else {}
    out = call("finish", kernel, ins, outs, scratch, 3 * 5 + 14, after, aliases)
    return out


def four_blocks(place, held, after):
    def items(at, refs):
        found = []
        for i, stream in enumerate((ONE, TWO)):
            for k in range(3):
                for e in range(4):
                    found.append((3 * i + k, e, refs[e * 3 + k].at[:, stream.place_of(k)]))
        for k in range(3):
            for e in range(4):
                to = pl.ds(sum(WIDTHS[:k]), WIDTHS[k])
                found.append((6, (e, slice(None), to), refs[e * 3 + k]))
        return found

    outs = [shape(4, ROWS, part.sent) for s in (ONE, TWO) for part in s.parts]
    outs.append(shape(4, ROWS, sum(WIDTHS)))
    out = copied("four", [place, *held], outs, items, after)
    return out[:3], out[3:6], out[6]


def multiplied(place, side, own, other, weight, total, stream, notes, after):
    last = bool(notes)
    half = NZ * NY * ROWS
    ins = [*own, *other, *notes]
    n = len(ins)
    more = [] if total is None else [total]

    def position(part, e1, e2, e3, c):
        z, y = part.apart(e1, e2, e3)
        return pl.ds((c * NZ * NY + z * NY + y) * ROWS, ROWS)

    def kernel(*refs):
        weight_ref = refs[n]
        at = n + 1 + len(more) + len(after)
        target = refs[at]
        rows, held, out, sems = refs[at + 1], refs[at + 2], refs[at + 3], refs[-1]
        copies = Copies(sems)
        loads = []
        for k, part in enumerate(stream.parts):
            columns = stream.local(k, True)
            half_depth = part.features // 2
            going = []
            for h in range(2):
                there = pl.ds(part.start + h * half_depth, half_depth)
                here = pl.ds(stream.offsets[k] + h * half_depth, half_depth)
                going.append(copies.start(weight_ref.at[there], held.at[here]))
            for e in range(4):
                to = rows.at[pl.ds(e * ROWS, ROWS), columns]
                going.append(copies.start(refs[k].at[e], to))
                source = refs[3 + k].at[e] if len(other) > 1 else refs[3].at[e, :, stream.beside(k)]
                to = rows.at[pl.ds((4 + e) * ROWS, ROWS), columns]
                going.append(copies.start(source, to))
            loads.append(going)
        if last:
            part = stream.parts[2]
            near, beside, notes_held = refs[n - 2], refs[n - 1], refs[at + 4]
            first = [
                copies.start(near.at[:, :, pl.ds(part.features, NOTE)], notes_held.at[0]),
                copies.start(beside.at[:, :, pl.ds(sum(WIDTHS) - NOTE, NOTE)], notes_held.at[1]),
            ]
        if more:
            before = copies.start(refs[n + 1], out)
        else:
            out[...] = jnp.zeros_like(out)
        for k, part in enumerate(stream.parts):
            half_depth = part.features // 2
            start = stream.offsets[k]
            for copy in [loads[k][0], *loads[k][2:]]:
                copy.wait()
            here = pl.ds(start, half_depth)
            product = jnp.dot(rows[:, here], held[here, :], preferred_element_type=jnp.float32)
            loads[k][1].wait()
            here = pl.ds(start + half_depth, half_depth)
            product += jnp.dot(rows[:, here], held[here, :], preferred_element_type=jnp.float32)
            if more and k == 0:
                before.wait()
            for c in range(NC):
                for e in range(4):
                    some = (c * 4 + e) * ROWS
                    out[position(part, side, e // 2, e % 2, c), :] += product[some : some + ROWS]
        if not last:
            copies.start(out, target).wait()
        else:
            for copy in first:
                copy.wait()
            part, place_now = stream.parts[2], where_am_i()
            for e1 in range(2):
                for e in range(4):
                    for c in range(NC):
                        if e1 == side:
                            some = pl.ds((c * 4 + e) * ROWS, ROWS)
                            note = rows[some, pl.ds(stream.features, NOTE)]
                        else:
                            note = notes_held[c, e]
                        scale = jnp.sum(note.astype(jnp.float32), axis=1, keepdims=True)
                        apart = part.apart(e1, e // 2, e % 2)
                        to = row_block(place_now, apart) * NC + lax.bitwise_xor(place_now[2], c)
                        to = pl.ds(pl.multiple_of(to * ROWS, ROWS), ROWS)
                        here = position(part, e1, e // 2, e % 2, c)
                        target[to, :] = bf16(out[here, :] * scale)

    scratch = [
        pltpu.VMEM((half, stream.features + stream.note), jnp.bfloat16),
        pltpu.VMEM((stream.features, COLS), jnp.bfloat16),
    ]
    scratch.append(pltpu.VMEM((2 * half, COLS), jnp.float32))
    if last:
        scratch.append(pltpu.VMEM((NC, 4, ROWS, NOTE), jnp.bfloat16))
    dtype = jnp.bfloat16 if last else jnp.float32
    return pl.pallas_call(
        kernel,
        in_specs=[ANY] * (n + 1 + len(more) + len(after)),
        name="multiply",
        out_specs=VMEM if last else ANY,
        out_shape=shape(2 * half, COLS, dtype=dtype),
        scratch_shapes=scratch + [pltpu.SemaphoreType.DMA((34,))],
        compiler_params=pltpu.CompilerParams(vmem_limit_bytes=PRODUCT_BYTES),
        cost_estimate=pl.CostEstimate(flops=0, bytes_accessed=1024, transcendentals=0),
    )(*ins, weight, *more, *after)


ORDERS = (("a", "b", "z"), ("b", "z", "a"), ("z", "a", "b"))


def streams_of(first, second, note):
    runs, start = ([], []), 0
    for k, dims in enumerate(ORDERS):
        runs[0].append(Part(start, first[k], dims))
        runs[1].append(Part(start + first[k], second[k], dims, note if k == 2 else 0))
        start += first[k] + second[k]
    return Stream(runs[0], (0, 0, 0)), Stream(runs[1], first)


FIRST, SECOND = streams_of((2560, 3584, 3584), (3072, 1536, 2048), NOTE)
ONE, TWO = streams_of((4096, 4096, 4096), (1536, 1024, 1536), NOTE)
WIDTHS = [a.sent + b.sent for a, b in zip(FIRST.parts, SECOND.parts)]


def per_device(partials, residual, norm_gain, qkv_weight):
    place = None
    terms = partials.reshape(NZ * NY * NC, ROWS, D)
    gain = norm_gain.astype(jnp.float32).reshape(1, D)

    def along(step, arrays):
        return [send(x, TO[ORDERS[k][step]]) for k, x in enumerate(arrays)]

    def across(arrays):
        return [send(x, TO_CORE) for x in arrays]

    a, b = FIRST, SECOND
    wanted = [(part, 1, a.offsets[k]) for k, part in enumerate(a.parts)]
    a_give = give(place, terms, wanted, a.features, [])
    a_got = across(a_give)[0]
    wanted = [(part, 0, part.start) for part in (*a.parts, *b.parts)]
    wanted += [(part, 1, D + b.offsets[k]) for k, part in enumerate(b.parts)]
    give_rest = give(place, terms, wanted, D + b.features, [a_give[0]])
    give_rest, _ = lax.optimization_barrier((give_rest[0], a_got))
    rest = send(give_rest, TO_CORE)
    a_out = first_step(place, terms, a_got, 0, a, [give_rest])
    a_one = along(0, a_out)
    b_out = first_step(place, terms, rest, D, b, [a_out[0]])
    b_one = along(0, b_out)
    a_out = second_step(place, terms, rest, a_one, a, [b_out[0]])
    a_two = along(1, a_out)
    b_out = second_step(place, terms, rest, b_one, b, [a_out[0]])
    b_two = along(1, b_out)
    a_out = third_step(place, terms, rest, a_one, a_two, a, [b_out[0]])
    a_three = along(2, a_out)
    b_out = third_step(place, terms, rest, b_one, b_two, b, [a_out[0]])
    b_three = along(2, b_out)
    so_far = finish(
        place, terms, rest, a_one, a_two, a_three, a, residual, gain, (), [b_out[0]]
    )
    stream, *rows, _ = finish(
        place, terms, rest, b_one, b_two, b_three, b, residual, gain, so_far, []
    )
    rows_z = along(2, rows)
    rows_y = along(1, rows)
    rows_zy = along(1, rows_z)
    held = [*rows, *rows_z, *rows_y, *rows_zy]
    a_near, b_near, beside = four_blocks(place, held, [])
    a_far = along(0, a_near)
    b_far = along(0, b_near)
    beside = send(beside, TO_CORE)

    near = functools.partial(multiplied, place, 0)
    far = functools.partial(multiplied, place, 1)
    total = near(a_near, [beside], qkv_weight, None, ONE, [], [])
    total = near(b_near, [beside], qkv_weight, total, TWO, [], [])
    *a_ready, _ = lax.optimization_barrier((*a_far, total))
    total = far(a_far, across(a_ready), qkv_weight, total, ONE, [], [])
    *b_ready, _ = lax.optimization_barrier((*b_far, total))
    notes = [b_near[2], beside]
    projected = far(b_far, across(b_ready), qkv_weight, total, TWO, notes, [])
    return stream, projected


def solution(mesh):
    in_specs = (P("tensor", "dp", None), P(("dp", "tensor"), None), P(), P(None, "tensor"))
    out_specs = (P(("dp", "tensor"), None), P("dp", "tensor"))
    return jax.shard_map(
        per_device, mesh=mesh, in_specs=in_specs, out_specs=out_specs, check_vma=False
    )
```

```python
import functools

import jax
import jax.numpy as jnp
from jax import lax
from jax.experimental import pallas as pl
from jax.experimental.pallas import tpu as pltpu
from jax.sharding import PartitionSpec as P

NZ, NY, NC = 2, 4, 2
ROWS = 32
D = 16384
COLS = 640
NOTE = 128
ANY = pl.BlockSpec(memory_space=pl.ANY)
VMEM = pl.BlockSpec(memory_space=pltpu.VMEM)
MIB = 1024 * 1024
SUM_BYTES = 45 * MIB
ROW_BYTES = 16 * MIB
PRODUCT_BYTES = 41 * MIB


def index_of(z, y, c):
    return (z * NY + y % NY) * NC + c


def pairs(move):
    return [
        (index_of(z, y, c), index_of(*move(z, y, c)))
        for z in range(NZ)
        for y in range(NY)
        for c in range(NC)
    ]


MOVES = {"a": (0, 1), "b": (0, 3), "z": (1, 0)}
TO = {d: pairs(lambda z, y, c, m=m: (z ^ m[0], y ^ m[1], c)) for d, m in MOVES.items()}
TO_CORE = pairs(lambda z, y, c: (z, y, 1 - c))


def send(x, where):
    return lax.ppermute(x, "tensor", where)


def bf16(x):
    return x.astype(jnp.bfloat16)


def shape(*dims, dtype=jnp.bfloat16):
    return jax.ShapeDtypeStruct(dims, dtype)


class Copies:
    def __init__(self, sems):
        self.sems, self.count = sems, 0

    def start(self, source, target):
        copy = pltpu.make_async_copy(source, target, self.sems.at[self.count])
        self.count += 1
        copy.start()
        return copy


def by_columns(width, body):
    step = 512 if width % 512 == 0 else 256

    def at(i, carry):
        return body(pl.ds(pl.multiple_of(i * step, step), step), carry)

    steps = width // step
    unroll = next(u for u in (3, 7, 5, 2, 1) if steps % u == 0)
    return functools.partial(lax.fori_loop, 0, steps, at, unroll=unroll)


def total_of(sources, columns):
    total = sources[0][:, columns].astype(jnp.float32)
    for ref in sources[1:]:
        total = total + ref[:, columns].astype(jnp.float32)
    return total


def where_am_i():
    t = lax.axis_index("tensor")
    return t // (NY * NC), t // NC % NY, t % NC


def call(name, kernel, ins, outs, scratch, copies, after, aliases={}, limit=SUM_BYTES):
    return pl.pallas_call(
        lambda *refs: kernel(where_am_i(), *refs),
        in_specs=[ANY] * (len(ins) - 1 + len(after)),
        out_specs=[ANY] * len(outs),
        name=name,
        out_shape=outs,
        scratch_shapes=scratch + [pltpu.SemaphoreType.DMA((copies,))],
        input_output_aliases=aliases,
        compiler_params=pltpu.CompilerParams(vmem_limit_bytes=limit),
        cost_estimate=pl.CostEstimate(flops=0, bytes_accessed=1024, transcendentals=0),
    )(*ins[1:], *after)


def copied(name, ins, outs, items, after):
    n = len(ins)

    def kernel(*refs):
        place, sources = refs[0], refs[1:n]
        targets, sems = refs[n + len(after) : -1], refs[-1]
        copies = Copies(sems)
        going = [
            copies.start(source, targets[k].at[index])
            for k, index, source in items(place, sources)
        ]
        for copy in going:
            copy.wait()

    return call(name, kernel, ins, outs, [], 36, after, limit=ROW_BYTES)


def added(name, ins, steps, others, stream, after):
    n, count = len(ins), len(steps)
    most = 1 + len(others([None] * n, 0))
    widest = max(part.features for part in stream.parts)

    def kernel(*refs):
        at, x, targets = refs[0], refs[1], refs[n + len(after) : n + len(after) + 3]
        taken, made, sems = refs[-3:]
        copies = Copies(sems)
        loads, storing = [], []
        for k, part in enumerate(stream.parts):
            inside = pl.ds(0, part.features)
            going = []
            for e, step in enumerate(steps):
                source = x.at[block(at, part.apart(*step), 0), :, part.columns]
                going.append(copies.start(source, taken.at[0, k, e, :, inside]))
            for j, source in enumerate(others(refs, k)):
                going.append(copies.start(source, taken.at[1 + j, k, :, :, inside]))
            loads.append(going)
        for k, part in enumerate(stream.parts):
            for copy in loads[k]:
                copy.wait()

            def one(e, carry, k=k, width=part.features):
                def body(columns, carry):
                    total = taken[0, k, e, :, columns].astype(jnp.float32)
                    for j in range(1, most):
                        total = total + taken[j, k, e, :, columns].astype(jnp.float32)
                    made[k, e, :, columns] = bf16(total)
                    return carry

                return by_columns(width, body)(carry)

            lax.fori_loop(0, count, one, 0)
            source = made.at[k, :, :, pl.ds(0, part.features)]
            storing.append(copies.start(source, targets[k]))
        for copy in storing:
            copy.wait()

    scratch = [
        pltpu.VMEM((most, 3, count, ROWS, widest), jnp.bfloat16),
        pltpu.VMEM((3, count, ROWS, widest), jnp.bfloat16),
    ]
    outs = [shape(count, ROWS, part.features) for part in stream.parts]
    return call(name, kernel, ins, outs, scratch, 3 * (count + most), after)


class Part:
    def __init__(self, start, features, dims, note=0):
        self.start, self.features, self.note = start, features, note
        self.sent = features + note
        self.columns = pl.ds(start, features)
        self.dims = dims

    def apart(self, *steps):
        z = y = 0
        for d, step in zip(self.dims, steps):
            if step:
                z, y = z ^ MOVES[d][0], y ^ MOVES[d][1]
        return z, y


class Stream:
    def __init__(self, parts, before):
        self.parts, self.before = parts, before
        self.features = sum(p.features for p in parts)
        self.note = sum(p.note for p in parts)
        self.offsets = [sum(p.features for p in parts[:k]) for k in range(len(parts))]

    def local(self, k, extra=False):
        return pl.ds(self.offsets[k], self.parts[k].sent if extra else self.parts[k].features)

    def beside(self, k):
        return pl.ds(sum(WIDTHS[:k]) + self.before[k], self.parts[k].sent)

    def place_of(self, k):
        return pl.ds(self.before[k], self.parts[k].sent)


def row_block(place, apart):
    z, y = place[0], place[1]
    return lax.bitwise_xor(z, apart[0]) * NY + lax.bitwise_xor(y, apart[1])


def block(place, apart, dc):
    c = place[2]
    return row_block(place, apart) * NC + lax.bitwise_xor(c, dc)


def give(place, terms, wanted, width, after):
    def items(at, x):
        return [
            (
                (e2 * 2 + e3, slice(None), pl.ds(position, part.features)),
                x.at[block(at, part.apart(first, e2, e3), 1), :, part.columns],
            )
            for part, first, position in wanted
            for e2 in (1, 0)
            for e3 in (0, 1)
        ]

    def kernel(*refs):
        at, x = refs[:2]
        target, held, sems = refs[-3:]
        copies = Copies(sems)
        todo = []
        for index, source in items(at, x):
            todo.append((index, copies.start(source, held.at[index])))
        storing = []
        for index, copy in todo:
            copy.wait()
            storing.append(copies.start(held.at[index], target.at[index]))
        for copy in storing:
            copy.wait()

    scratch = [pltpu.VMEM((4, ROWS, width), jnp.bfloat16)]
    out = shape(4, ROWS, width)
    return call("give", kernel, [place, terms], [out], scratch, 8 * len(wanted), after)


def from_core(ref, blocks, position, part):
    if ref is None:
        return None
    return ref.at[blocks, :, pl.ds(position, part.features)]


def pick(ref, index):
    return None if ref is None else ref.at[index]


QUARTERS = ((0, 0), (0, 1), (1, 0), (1, 1))


def first_step(place, terms, got, offset, stream, after):
    def others(refs, k):
        return [from_core(refs[2], pl.ds(0, 4), offset + stream.offsets[k], stream.parts[k])]

    steps = [(1, *q) for q in QUARTERS]
    return added("first", [place, terms, got], steps, others, stream, after)


def second_step(place, terms, rest, one, stream, after):
    def others(refs, k):
        some = pl.ds(2, 2)
        return [from_core(refs[2], some, stream.parts[k].start, stream.parts[k]), pick(refs[3 + k], some)]

    steps = [(0, 1, 0), (0, 1, 1)]
    return added("second", [place, terms, rest, *one], steps, others, stream, after)


def third_step(place, terms, rest, one, two, stream, after):
    def others(refs, k):
        some = pl.ds(1, 1)
        got = from_core(refs[2], some, stream.parts[k].start, stream.parts[k])
        return [got, pick(refs[3 + k], some), pick(refs[6 + k], some)]

    steps = [(0, 0, 1)]
    return added("third", [place, terms, rest, *one, *two], steps, others, stream, after)


def finish(place, terms, rest, one, two, three, stream, residual, gain, so_far, after):
    ins = [place, terms, rest, *one, *two, *three, residual, gain, *so_far]
    widest = max(part.features for part in stream.parts)

    def kernel(*refs):
        at, x = refs[0], refs[1]
        r, v, w, u = refs[2], refs[3:6], refs[6:9], refs[9:12]
        residual_ref, gain_ref = refs[12:14]
        base = len(ins) + len(after)
        stream_out, gained_out, squares_out = refs[base], refs[base + 1 : base + 4], refs[base + 4]
        taken, old, gains, news, made, sums, sems = refs[base + 5 :]
        copies = Copies(sems)
        first = []
        for k, part in enumerate(stream.parts):
            here = stream.local(k)
            first.append(copies.start(residual_ref.at[:, part.columns], old.at[:, here]))
            first.append(copies.start(gain_ref.at[:, part.columns], gains.at[:, here]))
        if so_far:
            first.append(copies.start(refs[18], sums))
        else:
            sums[...] = jnp.zeros_like(sums)
        loads, slots = [], []
        for k, part in enumerate(stream.parts):
            mine = x.at[block(at, part.apart(0, 0, 0), 0), :, part.columns]
            blocks = [mine, from_core(r, 0, part.start, part), v[k].at[0], w[k].at[0], u[k].at[0]]
            slots.append([taken.at[k, j, :, pl.ds(0, part.features)] for j in range(5)])
            loads.append([copies.start(b, s) for b, s in zip(blocks, slots[k])])
        for copy in first:
            copy.wait()
        total = sums[...]
        storing = []
        for k, part in enumerate(stream.parts):
            for copy in loads[k]:
                copy.wait()

            def body(columns, carry, k=k, offset=stream.offsets[k]):
                here = pl.ds(pl.multiple_of(offset + columns.start, 128), columns.size)
                x = total_of(slots[k], columns) + old[:, here].astype(jnp.float32)
                news[:, here] = bf16(x)
                made[k, :, columns] = bf16(x * gains[:, here])
                square = x * x
                return carry + sum(square[:, i : i + 128] for i in range(0, columns.size, 128))

            total = by_columns(part.features, body)(total)
            here = news.at[:, stream.local(k)]
            storing.append(copies.start(here, stream_out.at[:, part.columns]))
            if not part.note:
                here = made.at[k, :, pl.ds(0, part.features)]
                storing.append(copies.start(here, gained_out[k].at[:, stream.place_of(k)]))
        sums[...] = total
        storing.append(copies.start(sums, squares_out))
        for k, part in enumerate(stream.parts):
            if part.note:
                mean = jnp.sum(total, axis=1, keepdims=True) / D
                scale = jnp.broadcast_to(lax.rsqrt(mean + 1e-05), (ROWS, NOTE))
                high = bf16(scale).astype(jnp.float32)
                middle = bf16(scale - high).astype(jnp.float32)
                low = scale - high - middle
                lane = lax.broadcasted_iota(jnp.int32, (ROWS, NOTE), 1)
                parts = jnp.where(lane == 0, high, jnp.where(lane == 1, middle, low))
                made[k, :, pl.ds(part.features, NOTE)] = bf16(jnp.where(lane < 3, parts, 0.0))
                here = made.at[k, :, pl.ds(0, part.sent)]
                storing.append(copies.start(here, gained_out[k].at[:, stream.place_of(k)]))
        for copy in storing:
            copy.wait()

    outs = [shape(ROWS, D)]
    outs += [shape(ROWS, w) for w in WIDTHS]
    outs += [shape(ROWS, 128, dtype=jnp.float32)]
    scratch = [
        pltpu.VMEM((3, 5, ROWS, widest), jnp.bfloat16),
        pltpu.VMEM((ROWS, stream.features), jnp.bfloat16),
        pltpu.VMEM((1, stream.features), jnp.float32),
        pltpu.VMEM((ROWS, stream.features), jnp.bfloat16),
        pltpu.VMEM((3, ROWS, widest + NOTE), jnp.bfloat16),
        pltpu.VMEM((ROWS, 128), jnp.float32),
    ]
    aliases = {13: 0, 14: 1, 15: 2, 16: 3} if so_far else {}
    out = call("finish", kernel, ins, outs, scratch, 3 * 5 + 14, after, aliases)
    return out


def four_blocks(place, held, after):
    def items(at, refs):
        found = []
        for i, stream in enumerate((ONE, TWO)):
            for k in range(3):
                for e in range(4):
                    found.append((3 * i + k, e, refs[e * 3 + k].at[:, stream.place_of(k)]))
        for k in range(3):
            for e in range(4):
                to = pl.ds(sum(WIDTHS[:k]), WIDTHS[k])
                found.append((6, (e, slice(None), to), refs[e * 3 + k]))
        return found

    outs = [shape(4, ROWS, part.sent) for s in (ONE, TWO) for part in s.parts]
    outs.append(shape(4, ROWS, sum(WIDTHS)))
    out = copied("four", [place, *held], outs, items, after)
    return out[:3], out[3:6], out[6]


def multiplied(place, side, own, other, weight, total, stream, notes, after):
    last = bool(notes)
    half = NZ * NY * ROWS
    ins = [*own, *other, *notes]
    n = len(ins)
    more = [] if total is None else [total]

    def position(part, e1, e2, e3, c):
        z, y = part.apart(e1, e2, e3)
        return pl.ds((c * NZ * NY + z * NY + y) * ROWS, ROWS)

    def kernel(*refs):
        weight_ref = refs[n]
        at = n + 1 + len(more) + len(after)
        target = refs[at]
        rows, held, out, sems = refs[at + 1], refs[at + 2], refs[at + 3], refs[-1]
        copies = Copies(sems)
        loads = []
        for k, part in enumerate(stream.parts):
            columns = stream.local(k, True)
            half_depth = part.features // 2
            going = []
            for h in range(2):
                there = pl.ds(part.start + h * half_depth, half_depth)
                here = pl.ds(stream.offsets[k] + h * half_depth, half_depth)
                going.append(copies.start(weight_ref.at[there], held.at[here]))
            for e in range(4):
                to = rows.at[pl.ds(e * ROWS, ROWS), columns]
                going.append(copies.start(refs[k].at[e], to))
                source = refs[3 + k].at[e] if len(other) > 1 else refs[3].at[e, :, stream.beside(k)]
                to = rows.at[pl.ds((4 + e) * ROWS, ROWS), columns]
                going.append(copies.start(source, to))
            loads.append(going)
        if last:
            part = stream.parts[2]
            near, beside, notes_held = refs[n - 2], refs[n - 1], refs[at + 4]
            first = [
                copies.start(near.at[:, :, pl.ds(part.features, NOTE)], notes_held.at[0]),
                copies.start(beside.at[:, :, pl.ds(sum(WIDTHS) - NOTE, NOTE)], notes_held.at[1]),
            ]
        if more:
            before = copies.start(refs[n + 1], out)
        else:
            out[...] = jnp.zeros_like(out)
        for k, part in enumerate(stream.parts):
            half_depth = part.features // 2
            start = stream.offsets[k]
            depth = part.features if k else half_depth
            for copy in [loads[k][0], *loads[k][2:]]:
                copy.wait()
            if k:
                loads[k][1].wait()
            here = pl.ds(start, depth)
            product = jnp.dot(rows[:, here], held[here, :], preferred_element_type=jnp.float32)
            if not k:
                loads[k][1].wait()
                here = pl.ds(start + depth, depth)
                product += jnp.dot(rows[:, here], held[here, :], preferred_element_type=jnp.float32)
            if more and k == 0:
                before.wait()
            for c in range(NC):
                for e in range(4):
                    some = (c * 4 + e) * ROWS
                    out[position(part, side, e // 2, e % 2, c), :] += product[some : some + ROWS]
        if not last:
            copies.start(out, target).wait()
        else:
            for copy in first:
                copy.wait()
            part, place_now = stream.parts[2], where_am_i()
            for e1 in range(2):
                for e in range(4):
                    for c in range(NC):
                        if e1 == side:
                            some = pl.ds((c * 4 + e) * ROWS, ROWS)
                            note = rows[some, pl.ds(stream.features, NOTE)]
                        else:
                            note = notes_held[c, e]
                        scale = jnp.sum(note.astype(jnp.float32), axis=1, keepdims=True)
                        apart = part.apart(e1, e // 2, e % 2)
                        to = row_block(place_now, apart) * NC + lax.bitwise_xor(place_now[2], c)
                        to = pl.ds(pl.multiple_of(to * ROWS, ROWS), ROWS)
                        here = position(part, e1, e // 2, e % 2, c)
                        target[to, :] = bf16(out[here, :] * scale)

    scratch = [
        pltpu.VMEM((half, stream.features + stream.note), jnp.bfloat16),
        pltpu.VMEM((stream.features, COLS), jnp.bfloat16),
    ]
    scratch.append(pltpu.VMEM((2 * half, COLS), jnp.float32))
    if last:
        scratch.append(pltpu.VMEM((NC, 4, ROWS, NOTE), jnp.bfloat16))
    dtype = jnp.bfloat16 if last else jnp.float32
    return pl.pallas_call(
        kernel,
        in_specs=[ANY] * (n + 1 + len(more) + len(after)),
        name="multiply",
        out_specs=VMEM if last else ANY,
        out_shape=shape(2 * half, COLS, dtype=dtype),
        scratch_shapes=scratch + [pltpu.SemaphoreType.DMA((34,))],
        compiler_params=pltpu.CompilerParams(vmem_limit_bytes=PRODUCT_BYTES),
        cost_estimate=pl.CostEstimate(flops=0, bytes_accessed=1024, transcendentals=0),
    )(*ins, weight, *more, *after)


ORDERS = (("a", "b", "z"), ("b", "z", "a"), ("z", "a", "b"))


def streams_of(first, second, note):
    runs, start = ([], []), 0
    for k, dims in enumerate(ORDERS):
        runs[0].append(Part(start, first[k], dims))
        runs[1].append(Part(start + first[k], second[k], dims, note if k == 2 else 0))
        start += first[k] + second[k]
    return Stream(runs[0], (0, 0, 0)), Stream(runs[1], first)


FIRST, SECOND = streams_of((2560, 3584, 3584), (3072, 1536, 2048), NOTE)
ONE, TWO = streams_of((4096, 4096, 4096), (1536, 1024, 1536), NOTE)
WIDTHS = [a.sent + b.sent for a, b in zip(FIRST.parts, SECOND.parts)]


def per_device(partials, residual, norm_gain, qkv_weight):
    place = None
    terms = partials.reshape(NZ * NY * NC, ROWS, D)
    gain = norm_gain.astype(jnp.float32).reshape(1, D)

    def along(step, arrays):
        return [send(x, TO[ORDERS[k][step]]) for k, x in enumerate(arrays)]

    def across(arrays):
        return [send(x, TO_CORE) for x in arrays]

    a, b = FIRST, SECOND
    wanted = [(part, 1, a.offsets[k]) for k, part in enumerate(a.parts)]
    a_give = give(place, terms, wanted, a.features, [])
    a_got = across(a_give)[0]
    wanted = [(part, 0, part.start) for part in (*a.parts, *b.parts)]
    wanted += [(part, 1, D + b.offsets[k]) for k, part in enumerate(b.parts)]
    give_rest = give(place, terms, wanted, D + b.features, [a_give[0]])
    give_rest, _ = lax.optimization_barrier((give_rest[0], a_got))
    rest = send(give_rest, TO_CORE)
    a_out = first_step(place, terms, a_got, 0, a, [give_rest])
    a_one = along(0, a_out)
    b_out = first_step(place, terms, rest, D, b, [a_out[0]])
    b_one = along(0, b_out)
    a_out = second_step(place, terms, rest, a_one, a, [b_out[0]])
    a_two = along(1, a_out)
    b_out = second_step(place, terms, rest, b_one, b, [a_out[0]])
    b_two = along(1, b_out)
    a_out = third_step(place, terms, rest, a_one, a_two, a, [b_out[0]])
    a_three = along(2, a_out)
    b_out = third_step(place, terms, rest, b_one, b_two, b, [a_out[0]])
    b_three = along(2, b_out)
    so_far = finish(
        place, terms, rest, a_one, a_two, a_three, a, residual, gain, (), [b_out[0]]
    )
    stream, *rows, _ = finish(
        place, terms, rest, b_one, b_two, b_three, b, residual, gain, so_far, []
    )
    rows_z = along(2, rows)
    rows_y = along(1, rows)
    rows_zy = along(1, rows_z)
    held = [*rows, *rows_z, *rows_y, *rows_zy]
    a_near, b_near, beside = four_blocks(place, held, [])
    a_far = along(0, a_near)
    b_far = along(0, b_near)
    beside = send(beside, TO_CORE)

    near = functools.partial(multiplied, place, 0)
    far = functools.partial(multiplied, place, 1)
    total = near(a_near, [beside], qkv_weight, None, ONE, [], [])
    total = near(b_near, [beside], qkv_weight, total, TWO, [], [])
    *a_ready, _ = lax.optimization_barrier((*a_far, total))
    total = far(a_far, across(a_ready), qkv_weight, total, ONE, [], [])
    *b_ready, _ = lax.optimization_barrier((*b_far, total))
    notes = [b_near[2], beside]
    projected = far(b_far, across(b_ready), qkv_weight, total, TWO, notes, [])
    return stream, projected


def solution(mesh):
    in_specs = (P("tensor", "dp", None), P(("dp", "tensor"), None), P(), P(None, "tensor"))
    out_specs = (P(("dp", "tensor"), None), P("dp", "tensor"))
    return jax.shard_map(
        per_device, mesh=mesh, in_specs=in_specs, out_specs=out_specs, check_vma=False
    )
```
